256 devices in a mesh: dp: 64 (over x, z, core), inner: 4 (over y).
Axes of the slice: x: 4, y: 4, z: 8, core: 2. Of those that a mesh axis runs over, the one named last changes fastest.
Arguments:
- history: bfloat16 [32768, 1024], P('dp', 'inner'), may hold values from -6 to 6
- out_grad: bfloat16 [32768, 1024], P('dp', 'inner'), may hold values from -16 to 16
- lengths: int32 [64, 8], P('dp'), may hold values from 1 to 256, 512 in all within a row
- w_in: bfloat16 [1024, 4096], P('dp', 'inner'), may hold values from -0.1875 to 0.1875
- w_out: bfloat16 [1024, 1024], P('inner', 'dp'), may hold values from -0.1875 to 0.1875
Outputs:
- output: bfloat16 [32768, 1024], P('dp', 'inner')
- grad_input: float32 [32768, 1024], P('dp', 'inner')
- grad_w_in: float32 [1024, 4096], P('dp', 'inner')
- grad_w_out: float32 [1024, 1024], P('inner', 'dp')
The draws below stay inside these ranges and needn't reach their ends.
Inputs may be any that keep to these rules, and one draw needn't show every extreme that they name: `lengths`: each row sums to 512; the longest history of every row is exactly 256.
All inputs are finite; a program needn't handle non-finite values.
Results may differ from the reference program's by a relative error of at most 0.01.
Values may be sent and summed in bfloat16 or wider, within the bound.
A program may use at most 64 MiB of HBM per device.

```python
import math
import jax
import jax.numpy as jnp
import numpy as np
from jax import lax

D = 1024
H = 8
DH = 128
TOK_DEV = 512
HIST_DEV = 8
MAXLEN = 256
TOKENS = 32768
N_DP = 64


def raised(result, own_key, source, target, blocks, factor):
    def block_of(dim):
        return (jnp.arange(result.shape[dim]) // (result.shape[dim] // blocks)).reshape((-1,) + (1,) * (result.ndim - 1 - dim))

    first = jax.random.permutation(own_key, blocks)[block_of(target)]
    far = (block_of(target) + blocks // 2) % blocks
    return jnp.where((block_of(source) == first) | (block_of(source) == far), factor * result, result)


def levels(own_key, extent, cuts, low, top_value):
    loudness = 1.0
    for axis_at, parts in cuts:
        steps = jax.random.uniform(jax.random.fold_in(jax.random.fold_in(own_key, 6), axis_at), (parts,), jnp.float32, low / len(cuts), top_value / len(cuts))
        loudness = loudness * jnp.repeat(jnp.exp(steps), extent[axis_at] // parts).reshape((-1,) + (1,) * (len(extent) - 1 - axis_at))
    return loudness


def length_profile(amount, total, bound, skew):
    portions = [(1 << 20) // math.isqrt(rank ** skew) + 1 for rank in range(2, amount + 1)]
    surplus, counts = total - bound - (amount - 1), [1] * (amount - 1)
    while surplus > 0:
        movable = [i for i in range(amount - 1) if counts[i] < bound]
        whole, remaining = sum([portions[i] for i in movable]), surplus
        for i in movable:
            more = min(bound - counts[i], max(1, remaining * portions[i] // whole), surplus)
            counts[i] = counts[i] + more
            surplus = surplus - more
    return np.array([bound] + counts)


def ragged_sizes(key, number_of, total, most, lean):
    if number_of == 2:
        one = jax.random.randint(key, (), max(1, total - most), min(most, total - 1) + 1)
        return jnp.stack([one, total - one])
    sizes = jnp.asarray(length_profile(number_of, total, most, lean), jnp.int32)
    pairs = (number_of - 1) // 2
    source_of, receiver = sizes[1:1 + 2 * pairs:2], sizes[2:2 + 2 * pairs:2]
    slack = jnp.minimum(source_of - 1, most - receiver)
    shifted = jax.random.randint(jax.random.fold_in(key, 1), (pairs,), 0, 1 << 20) % (slack + 1)
    sizes = sizes.at[1:1 + 2 * pairs:2].set(source_of - shifted).at[2:2 + 2 * pairs:2].set(receiver + shifted)
    return sizes[jax.random.permutation(jax.random.fold_in(key, 2), number_of)]


def centred(stream_key, dims, width, limit, cuts=(), held_as=jnp.bfloat16):
    drawn = jax.random.normal(stream_key, dims, jnp.float32) * width
    if len(cuts) > 0:
        drawn = levels(stream_key, dims, cuts, -0.22, 0.18) * drawn
    return jnp.clip(drawn, min=-limit, max=limit).astype(held_as)


def heavy_noise(stream_key, shape, scale, reach, split, heavy, held_as=jnp.bfloat16):
    result = scale * jax.random.normal(stream_key, shape, jnp.float32)
    if split:
        result = result * levels(stream_key, shape, split, -0.22, 0.18)
    return jnp.clip(raised(result, jax.random.fold_in(stream_key, 3), *heavy), -reach, reach).astype(held_as)


def setup_inputs(seed: int = 0) -> dict:
    splits = jax.random.split(jax.random.key(seed), 6)
    history = centred(splits[0], (TOKENS, D), 1.0, 6.0, ((0, 64), (1, 4)))
    out_grad = heavy_noise(splits[1], (TOKENS, D), 1.0, 16.0, ((0, 64), (1, 4)), (0, 1, 64, 4.0))
    lengths = jax.vmap(lambda own: ragged_sizes(own, HIST_DEV, TOK_DEV, TOK_DEV // 2, 2))(jax.random.split(splits[2], N_DP)).reshape((N_DP, HIST_DEV)).astype(jnp.int32)
    w_in = centred(splits[3], (D, H * 4 * DH), D ** -0.5, 0.1875, ((0, 64), (1, 4)))
    w_out = centred(splits[4], (H * DH, D), (H * DH) ** -0.5, 0.1875, ((0, 4), (1, 64)))
    return {"history": history, "out_grad": out_grad, "lengths": lengths, "w_in": w_in, "w_out": w_out}


EPSILON = 1e-06

def silu_slope(value_in):
    sigma = jax.nn.sigmoid(value_in)
    return sigma * (1.0 + value_in * (1.0 - sigma))

def normalize(values):
    row_mean = lax.optimization_barrier(jnp.mean(values, -1, keepdims=True))
    square_mean = lax.optimization_barrier(jnp.mean(values * values, -1, keepdims=True))
    inverse = lax.rsqrt(square_mean - row_mean * row_mean + EPSILON)
    return ((values - row_mean) * inverse, inverse)

def block_mask(length_row, row_count):
    seg_ends = jnp.cumsum(length_row).astype(jnp.int32)
    position = jnp.arange(row_count, dtype=jnp.int32)
    segment = lax.optimization_barrier(jnp.sum((position[:, None] >= seg_ends[None, :]).astype(jnp.int32), 1))
    return (segment[:, None] == segment[None, :]) & (position[:, None] >= position[None, :])

def one_block(block_in, block_grad, length_row, w_in, w_out):
    row_count = block_in.shape[0]
    input_f = block_in.astype(jnp.float32)
    normed_in, inverse_in = normalize(input_f)
    normed_bf = normed_in.astype(jnp.bfloat16)
    hidden = jnp.dot(normed_bf, w_in, preferred_element_type=jnp.float32)
    activated = jax.nn.silu(hidden).astype(jnp.bfloat16).reshape(row_count, H, 4, DH).astype(jnp.float32)
    gates = activated[:, :, 0]
    values_v = activated[:, :, 1]
    queries = activated[:, :, 2]
    key_rows = activated[:, :, 3]
    allowed = block_mask(length_row, row_count)
    score_scale = DH ** (-0.5)
    scores = jnp.einsum('qhd,khd->hqk', queries, key_rows) * score_scale
    weights_a = jnp.where(allowed, jax.nn.silu(scores) / MAXLEN, 0.0).astype(jnp.bfloat16).astype(jnp.float32)
    attended = jnp.einsum('hqk,khd->qhd', weights_a, values_v).reshape(row_count, H * DH)
    att_norm, att_inverse = normalize(attended)
    gate_flat = gates.reshape(row_count, H * DH)
    gated = (att_norm * gate_flat).astype(jnp.bfloat16)
    output = (input_f + jnp.dot(gated, w_out, preferred_element_type=jnp.float32)).astype(jnp.bfloat16)
    grad_gated = jnp.dot(block_grad, w_out.T, preferred_element_type=jnp.float32)
    w_out_term = jnp.dot(gated.T, block_grad, preferred_element_type=jnp.float32)
    grad_gate = grad_gated * att_norm
    grad_norm = grad_gated * gate_flat
    grad_att = (grad_norm - lax.optimization_barrier(jnp.mean(grad_norm, 1, keepdims=True)) - att_norm * lax.optimization_barrier(jnp.mean(grad_norm * att_norm, 1, keepdims=True))) * att_inverse
    grad_att = grad_att.astype(jnp.bfloat16).reshape(row_count, H, DH).astype(jnp.float32)
    grad_weights = jnp.einsum('qhd,khd->hqk', grad_att, values_v)
    grad_values = jnp.einsum('hqk,qhd->khd', weights_a, grad_att)
    grad_scores = jnp.where(allowed, grad_weights * silu_slope(scores) / MAXLEN, 0.0).astype(jnp.bfloat16).astype(jnp.float32)
    grad_queries = score_scale * jnp.einsum('hqk,khd->qhd', grad_scores, key_rows)
    grad_keys = score_scale * jnp.einsum('hqk,qhd->khd', grad_scores, queries)
    stacked = jnp.stack([grad_gate.reshape(row_count, H, DH), grad_values, grad_queries, grad_keys], 2)
    grad_hidden = (stacked.reshape(row_count, H * 4 * DH) * silu_slope(hidden)).astype(jnp.bfloat16)
    w_in_term = jnp.dot(normed_bf.T, grad_hidden, preferred_element_type=jnp.float32)
    grad_normed = jnp.dot(grad_hidden, w_in.T, preferred_element_type=jnp.float32)
    grad_input = block_grad.astype(jnp.float32) + (grad_normed - lax.optimization_barrier(jnp.mean(grad_normed, 1, keepdims=True)) - normed_in * lax.optimization_barrier(jnp.mean(grad_normed * normed_in, 1, keepdims=True))) * inverse_in
    return (output, grad_input, w_in_term, w_out_term)

def reference(history, out_grad, lengths, w_in, w_out):
    blocks = lengths.shape[0]
    history_blocks = history.reshape(blocks, -1, D)
    grad_blocks = out_grad.reshape(blocks, -1, D)

    def advance(totals, inputs_now):
        output, grad_input, w_in_term, w_out_term = one_block(inputs_now[0], inputs_now[1], inputs_now[2], w_in, w_out)
        return ((totals[0] + w_in_term, totals[1] + w_out_term), (output, grad_input))
    start_sums = (jnp.zeros(w_in.shape, jnp.float32), jnp.zeros(w_out.shape, jnp.float32))
    sums_out, results = lax.scan(advance, start_sums, (history_blocks, grad_blocks, lengths))
    return (results[0].reshape(-1, D), results[1].reshape(-1, D), sums_out[0], sums_out[1])
```

```python
import functools

import jax
import jax.numpy as jnp
from jax import lax
from jax.experimental import pallas as pl
from jax.experimental.pallas import tpu as pltpu
from jax.sharding import PartitionSpec as P

H = 8
DH = 128
MAXLEN = 256
EPSILON = 1e-06
SCALE = DH ** (-0.5)
F32 = jnp.float32
BF16 = jnp.bfloat16
NX = 4
NY = 4
N_SEM = 320

WO, GATE, QUERY, KEY, VALUE, COLS = 0, 256, 512, 768, 1024, 1280
EARLY_A, EARLY_B = (0, 256), (256, 512)
LATE_A, LATE_B = (512, 896), (896, 1280)


def nn(a, b):
    return lax.dot_general(a, b, (((1,), (0,)), ((), ())), preferred_element_type=F32)


def nt(a, b):
    return lax.dot_general(a, b, (((1,), (1,)), ((), ())), preferred_element_type=F32)


def tn(a, b):
    return lax.dot_general(a, b, (((0,), (0,)), ((), ())), preferred_element_type=F32)


class Links:
    def __init__(self, send_sem, recv_sem):
        self.send_sem, self.recv_sem, self.used, self.sent = send_sem, recv_sem, 0, []

    def send(self, source, target, device):
        index = self.used
        self.used += 1
        copy = pltpu.make_async_remote_copy(
            src_ref=source,
            dst_ref=target,
            send_sem=self.send_sem.at[index],
            recv_sem=self.recv_sem.at[index],
            device_id=device,
            device_id_type=pl.DeviceIdType.MESH,
        )
        copy.start()
        self.sent.append((copy, index))
        return index, device

    def arrived(self, handle, region):
        index, device = handle
        pltpu.make_async_remote_copy(
            src_ref=region,
            dst_ref=region,
            send_sem=self.send_sem.at[index],
            recv_sem=self.recv_sem.at[index],
            device_id=device,
            device_id_type=pl.DeviceIdType.MESH,
        ).wait_recv()

    def drain(self):
        for copy, _ in self.sent:
            copy.wait_send()


class RingGather:
    def __init__(self, links, view, right, left, source=None):
        self.links, self.view, self.right, self.left = links, view, right, left
        self.source = source or (lambda half: view(0, half))

    def start(self):
        send, view, source = self.links.send, self.view, self.source
        self.r0 = send(source(0), view(0, 0), self.right)
        self.l1 = send(source(1), view(0, 1), self.left)
        self.r1 = send(source(1), view(0, 1), self.right)
        self.l0 = send(source(0), view(0, 0), self.left)

    def forward(self):
        links, view = self.links, self.view
        links.arrived(self.r0, view(3, 0))
        self.fr = links.send(view(3, 0), view(3, 0), self.right)
        links.arrived(self.l1, view(1, 1))
        self.fl = links.send(view(1, 1), view(1, 1), self.left)

    def near(self):
        links, view = self.links, self.view
        links.arrived(self.r1, view(3, 1))
        links.arrived(self.l0, view(1, 0))

    def far(self):
        links, view = self.links, self.view
        links.arrived(self.fr, view(2, 0))
        links.arrived(self.fl, view(2, 1))


class RingSum:
    def __init__(self, links, part, out_buf, in_buf, right, left):
        self.links, self.part, self.out, self.inn = links, part, out_buf, in_buf
        self.right, self.left = right, left

    def push(self, slot, value, device):
        self.out[slot] = value.astype(BF16)
        return self.links.send(self.out.at[slot], self.inn.at[slot], device)

    def start_far(self):
        self.h0 = self.push(0, self.part(2, 0), self.right)
        self.h1 = self.push(1, self.part(2, 1), self.left)

    def start_right(self):
        self.h2 = self.push(2, self.part(1, 1), self.right)

    def start_left(self):
        self.h3 = self.push(3, self.part(3, 0), self.left)

    def middle(self):
        self.links.arrived(self.h0, self.inn.at[0])
        self.h4 = self.push(4, self.inn[0].astype(F32) + self.part(1, 0), self.right)
        self.links.arrived(self.h1, self.inn.at[1])
        self.h5 = self.push(5, self.inn[1].astype(F32) + self.part(3, 1), self.left)

    def finish(self):
        for handle, slot in ((self.h2, 2), (self.h3, 3), (self.h4, 4), (self.h5, 5)):
            self.links.arrived(handle, self.inn.at[slot])
        first = self.part(0, 0) + self.inn[4].astype(F32) + self.inn[3].astype(F32)
        second = self.part(0, 1) + self.inn[2].astype(F32) + self.inn[5].astype(F32)
        return first, second


def kernel(
    nz,
    history,
    out_grad,
    lengths,
    w_in,
    w_out,
    output,
    grad_input,
    grad_w_in,
    grad_w_out,
    xg,
    dg,
    xh,
    xt,
    dt,
    wg,
    hid,
    slope,
    act,
    mask,
    weights,
    sslope,
    att,
    gg,
    ga,
    gated,
    gh,
    sgrad,
    term,
    sib_out,
    sib_in,
    oterm,
    iterm,
    row_stat,
    st_own,
    st_in,
    st2_own,
    st2_in,
    yo_out,
    yo_in,
    yi_out,
    yi_in,
    wo_tmp,
    wo_back,
    ax_e,
    az_e,
    bz_e,
    bx_e,
    ax_l,
    az_l,
    bz_l,
    bx_l,
    send_sem,
    recv_sem,
    local_sem,
):
    tok, share = history.shape
    half_tok = tok // 2
    width = share * NY
    me = lax.axis_index("dp")
    y = lax.axis_index("inner")
    core = lax.rem(me, 2)
    z = lax.rem(lax.div(me, 2), nz)
    x = lax.div(me, 2 * nz)
    other = 1 - core

    def at_x(k):
        return lax.rem(x + k, NX)

    def at_z(k):
        return lax.rem(z + k, nz)

    def at_y(k):
        return lax.rem(y + k, NY)

    def dev_x(k):
        return {"dp": (at_x(k) * nz + z) * 2 + core}

    def dev_z(k):
        return {"dp": (x * nz + at_z(k)) * 2 + core}

    def dev_y(k):
        return {"inner": at_y(k)}

    sibling = {"dp": (x * nz + z) * 2 + other}
    links = Links(send_sem, recv_sem)

    barrier = pltpu.get_barrier_semaphore()
    partners = (
        [sibling]
        + [dev_y(k) for k in (1, 2, 3)]
        + [dev_x(k) for k in (1, 2, 3)]
        + [dev_z(k) for k in range(1, nz)]
    )
    for device in partners:
        pl.semaphore_signal(barrier, inc=1, device_id=device, device_id_type=pl.DeviceIdType.MESH)

    own_x = pltpu.make_async_copy(history, xg.at[y], local_sem.at[0])
    own_d = pltpu.make_async_copy(out_grad, dg.at[y], local_sem.at[1])
    own_x.start()
    own_d.start()
    wo_tmp[...] = jnp.zeros(wo_tmp.shape, F32)
    wo_tmp[:, 0:16] = w_out[...].astype(F32)
    mine = (x, z, core)
    wg[mine + (slice(None), slice(WO, WO + 256))] = wo_tmp[...].T[0:16, :].astype(BF16)
    for head in range(2):
        for part, base in enumerate((GATE, VALUE, QUERY, KEY)):
            source = head * 4 * DH + part * DH
            target = base + head * DH
            wg[mine + (slice(None), slice(target, target + DH))] = w_in[:, source : source + DH]
    pl.semaphore_wait(barrier, len(partners))

    def rows_of(half):
        return pl.ds(half * half_tok, half_tok)

    gather_x = RingGather(
        links,
        lambda k, half: xg.at[at_y(k), rows_of(half)],
        dev_y(1),
        dev_y(3),
        lambda half: history.at[rows_of(half)],
    )
    gather_d = RingGather(
        links,
        lambda k, half: dg.at[at_y(k), rows_of(half)],
        dev_y(1),
        dev_y(3),
        lambda half: out_grad.at[rows_of(half)],
    )

    n_right = nz // 2
    n_left = nz - 1 - n_right

    class WeightGather:
        def __init__(self, a, b):
            self.ca, self.cb = pl.ds(a[0], a[1] - a[0]), pl.ds(b[0], b[1] - b[0])
            self.shared = []

        def share(self, view):
            region = view(core)
            self.shared.append((links.send(region, region, sibling), view(other)))

        def start(self):
            own_b = wg.at[x, z, core, :, self.cb]
            own_a = wg.at[x, z, core, :, self.ca]
            self.bx = [links.send(own_b, own_b, dev_x(k)) for k in (1, 3, 2)]
            self.az = [(k, links.send(own_a, own_a, dev_z(k))) for k in range(1, nz)]

        def slab_b(self, zz, cc):
            return wg.at[:, zz, cc, :, self.cb]

        def start_b(self):
            for k, handle in zip((1, 3, 2), self.bx):
                links.arrived(handle, wg.at[at_x(NX - k), z, core, :, self.cb])
            region = self.slab_b(z, core)
            self.right = links.send(region, region, dev_z(1))
            if n_left:
                self.left = links.send(region, region, dev_z(nz - 1))
            self.share(lambda cc: self.slab_b(z, cc))
            self.step = 0

        def step_b(self):
            s = self.step
            self.step += 1
            if s < n_right:
                zz = at_z(nz - 1 - s)
                region = self.slab_b(zz, core)
                links.arrived(self.right, region)
                if s + 1 < n_right:
                    self.right = links.send(region, region, dev_z(1))
                self.share(lambda cc: self.slab_b(zz, cc))
            if s < n_left:
                zl = at_z(1 + s)
                region = self.slab_b(zl, core)
                links.arrived(self.left, region)
                if s + 1 < n_left:
                    self.left = links.send(region, region, dev_z(nz - 1))
                self.share(lambda cc: self.slab_b(zl, cc))

        def view_a(self, k, half, cc):
            return wg.at[at_x(k), pl.ds(half * (nz // 2), nz // 2), cc, :, self.ca]

        def start_a(self):
            for k, handle in self.az:
                links.arrived(handle, wg.at[x, at_z(nz - k), core, :, self.ca])
            self.ring = RingGather(
                links, lambda k, half: self.view_a(k, half, core), dev_x(1), dev_x(3)
            )
            self.ring.start()
            self.share(lambda cc: wg.at[x, :, cc, :, self.ca])

        def forward_a(self):
            self.ring.forward()
            self.share(lambda cc: self.view_a(3, 0, cc))
            self.share(lambda cc: self.view_a(1, 1, cc))

        def near_a(self):
            self.ring.near()
            self.share(lambda cc: self.view_a(3, 1, cc))
            self.share(lambda cc: self.view_a(1, 0, cc))

        def far_a(self):
            self.ring.far()
            self.share(lambda cc: self.view_a(2, 0, cc))
            self.share(lambda cc: self.view_a(2, 1, cc))

        def finish(self):
            for handle, region in self.shared:
                links.arrived(handle, region)

    late = WeightGather(LATE_A, LATE_B)
    early = WeightGather(EARLY_A, EARLY_B)
    gather_x.start()
    late.start()
    early.start()

    blocks = tok // 128
    ends = []
    total = jnp.int32(0)
    for k in range(8):
        total = total + lengths[0, k]
        ends.append(total)
    for i in range(blocks):
        row = lax.broadcasted_iota(jnp.int32, (128, 128), 0) + i * 128
        begin = jnp.zeros((128, 128), jnp.int32)
        for k in range(7):
            begin = jnp.where(row >= ends[k], ends[k], begin)
        for j in range(max(0, i - 2), i + 1):
            col = lax.broadcasted_iota(jnp.int32, (128, 128), 1) + j * 128
            allowed = (col >= begin) & (col <= row)
            mask[i * 128 : (i + 1) * 128, j * 128 : (j + 1) * 128] = jnp.where(
                allowed, 1.0 / MAXLEN, 0.0
            ).astype(F32)

    late.start_b()
    late.start_a()
    gather_x.forward()
    early.start_b()
    early.start_a()
    late.step_b()
    late.forward_a()
    own_x.wait()
    gather_x.near()
    gather_x.far()
    gather_d.start()
    late.step_b()

    def norm_rows(block, carry):
        rows = pl.ds(pl.multiple_of(block * 128, 128), 128)
        cols = [xg[k, rows, :].astype(F32) for k in range(NY)]
        mean = sum(jnp.sum(part, 1, keepdims=True) for part in cols) / width
        square = sum(jnp.sum(part * part, 1, keepdims=True) for part in cols) / width
        inverse = lax.rsqrt(square - mean * mean + EPSILON)
        row_stat[0, rows, :] = jnp.broadcast_to(mean, (128, 128))
        row_stat[1, rows, :] = jnp.broadcast_to(inverse, (128, 128))
        for k in range(NY):
            xh[rows, k * share : (k + 1) * share] = ((cols[k] - mean) * inverse).astype(BF16)
        return carry

    lax.fori_loop(0, blocks, norm_rows, 0)
    late.near_a()
    late.step_b()
    early.step_b()
    early.forward_a()
    for k in range(NX):
        turned = xh[:, k * share : (k + 1) * share].T
        xt[k] = turned.reshape(nz, 2, 16, tok)
    late.far_a()
    late.step_b()
    late.finish()
    early.step_b()
    early.near_a()

    def weight_cols(first, count):
        return wg[:, :, :, :, pl.ds(first, count)].reshape(width, count)

    def hidden_cols(chunk, carry):
        base = pl.multiple_of(chunk * 256, 256)
        block = wg[:, :, :, :, pl.ds(pl.multiple_of(base + GATE, 256), 256)].reshape(width, 256)
        for half in range(2):
            rows = pl.ds(half * half_tok, half_tok)
            value = nn(xh[rows, :], block)
            sigma = jax.nn.sigmoid(value)
            cols = pl.ds(base, 256)
            hid[rows, cols] = value
            act[rows, cols] = (value * sigma).astype(BF16)
            slope[rows, cols] = sigma * (1.0 + value * (1.0 - sigma))
        return carry

    lax.fori_loop(1, 4, hidden_cols, 0)
    gather_d.forward()
    early.step_b()
    early.far_a()
    early.step_b()

    def part_of(ref, base, head, rows):
        first = base - GATE + head * DH
        return ref[rows, first : first + DH]

    def band(i):
        return slice(i * 128, (i + 1) * 128), slice(max(0, i - 2) * 128, (i + 1) * 128)

    for head in range(2):
        for i in range(blocks):
            rows, cols = band(i)
            score = nt(part_of(act, QUERY, head, rows), part_of(act, KEY, head, cols)) * SCALE
            sigma = jax.nn.sigmoid(score)
            seen = mask[rows, cols]
            soft = score * sigma
            weight = (soft * seen).astype(BF16)
            weights[head, rows, cols] = weight
            sslope[head, rows, cols] = sigma * (1.0 + score * (1.0 - sigma)) * seen
            att[rows, head * DH : (head + 1) * DH] = nn(weight, part_of(act, VALUE, head, cols))

    early.finish()
    lax.fori_loop(0, 1, hidden_cols, 0)
    own_d.wait()
    gather_d.near()
    gather_d.far()
    for half in range(2):
        rows = pl.ds(half * half_tok, half_tok)
        total_gg = None
        for k in range(NY):
            block = wg[k, :, :, :, WO : WO + 256].reshape(share, 256)
            piece = nn(dg[k, rows, :], block)
            total_gg = piece if total_gg is None else total_gg + piece
        gg[rows, :] = total_gg

    def columns_sum(value):
        return jnp.sum(value.T, 0, keepdims=True)

    def gate_of(head):
        return part_of(act, GATE, head, slice(None)).astype(F32)

    def head_cols(head):
        return slice(head * DH, (head + 1) * DH)

    sums = [0.0] * 4
    for head in range(2):
        a = att[:, head_cols(head)]
        g = gg[:, head_cols(head)] * gate_of(head)
        for k, term_k in enumerate((a, a * a, g, g * a)):
            sums[k] = sums[k] + term_k
    for k in range(4):
        st_own[k : k + 1, :] = columns_sum(sums[k])
    stat = [(k, links.send(st_own, st_in.at[y], dev_y(k))) for k in (1, 3, 2)]
    for k in range(NY):
        dt[k] = dg[k].T.reshape(nz, 2, 16, tok)
    for k, handle in stat:
        links.arrived(handle, st_in.at[at_y(NY - k)])
    st_in[y] = st_own[...]
    sums = st_in[0] + st_in[1] + st_in[2] + st_in[3]

    def spread(row_values):
        return jnp.broadcast_to(row_values, (128, tok)).T

    att_mean = sums[0:1] / (H * DH)
    att_inv = lax.rsqrt(sums[1:2] / (H * DH) - att_mean * att_mean + EPSILON)
    norm_mean = sums[2:3] / (H * DH)
    cross_mean = (sums[3:4] - att_mean * sums[2:3]) * att_inv / (H * DH)
    att_mean, att_inv, norm_mean, cross_mean = (
        spread(value) for value in (att_mean, att_inv, norm_mean, cross_mean)
    )
    for head in range(2):
        cols = head_cols(head)
        att_norm = (att[:, cols] - att_mean) * att_inv
        gate = gate_of(head)
        gated[:, cols] = (att_norm * gate).astype(BF16)
        g = gg[:, cols]
        gh[:, cols] = (g * att_norm * slope[:, cols]).astype(BF16)
        ga[:, cols] = ((g * gate - norm_mean - att_norm * cross_mean) * att_inv).astype(BF16)

    class WeightSum:
        def __init__(self, a, b, ax, az, bz, bx):
            self.first, self.end = a[0], b[1]
            self.a, self.b = a, b
            self.wa, self.wb = a[1] - a[0], b[1] - b[0]
            self.ca, self.cb = slice(*a), slice(*b)
            self.ax, self.az, self.bz, self.bx = ax, az, bz, bx
            self.pairs = []

        def multiply(self, lhs, rhs, first):
            count = rhs.shape[1]
            cols = slice(first, first + count)
            for parity, own in ((other, False), (core, True)):
                rows = lhs[:, :, parity].reshape(width // 2, tok)
                value = nn(rows, rhs).reshape(NX, nz, 16, count)
                if own:
                    term[:, :, :, cols] = value
                else:
                    sib_out[:, :, :, cols] = value.astype(BF16)
                    view = (slice(None), slice(None), slice(None), cols)
                    handle = links.send(sib_out.at[view], sib_in.at[view], sibling)
                    self.pairs.append((handle, view))

        def join(self):
            for handle, view in self.pairs:
                links.arrived(handle, sib_in.at[view])
                term[view] = term[view] + sib_in[view].astype(F32)

        def part_a(self, k, half):
            return term[at_x(k), half * (nz // 2) : (half + 1) * (nz // 2), :, self.ca]

        def part_b(self, k):
            return term[:, at_z(k), :, self.cb]

        def start(self):
            self.ring = RingSum(
                links, self.part_a, self.ax.at[0], self.ax.at[1], dev_x(1), dev_x(3)
            )
            self.ring.start_far()
            self.step = 0
            self.push_right(self.part_b(n_right))
            if n_left:
                self.push_left(self.part_b(nz - n_left))
            self.ring.start_right()
            self.ring.start_left()

        def push_right(self, value):
            s = self.step
            self.bz[0, s] = value.astype(BF16)
            self.right = links.send(self.bz.at[0, s], self.bz.at[1, s], dev_z(1))

        def push_left(self, value):
            s = n_right + self.step
            self.bz[0, s] = value.astype(BF16)
            self.left = links.send(self.bz.at[0, s], self.bz.at[1, s], dev_z(nz - 1))

        def step_b(self):
            s = self.step
            self.step += 1
            if s + 1 < n_right:
                links.arrived(self.right, self.bz.at[1, s])
                self.push_right(self.bz[1, s].astype(F32) + self.part_b(n_right - s - 1))
            if s + 1 < n_left:
                links.arrived(self.left, self.bz.at[1, n_right + s])
                self.push_left(
                    self.bz[1, n_right + s].astype(F32) + self.part_b(nz - n_left + s + 1)
                )

        def middle_a(self):
            self.ring.middle()

        def turn_b(self):
            links.arrived(self.right, self.bz.at[1, n_right - 1])
            value = self.part_b(0) + self.bz[1, n_right - 1].astype(F32)
            if n_left:
                links.arrived(self.left, self.bz.at[1, n_right + n_left - 1])
                value = value + self.bz[1, n_right + n_left - 1].astype(F32)
            term[:, z, :, self.cb] = value
            self.hx = []
            for k in (2, 1, 3):
                self.bx[0, k] = term[at_x(k), z, :, self.cb].astype(BF16)
                self.hx.append((k, links.send(self.bx.at[0, k], self.bx.at[1, k], dev_x(k))))

        def turn_a(self):
            first, second = self.ring.finish()
            term[x, 0 : nz // 2, :, self.ca] = first
            term[x, nz // 2 : nz, :, self.ca] = second
            self.hz = []
            for d in range(nz // 2, 0, -1):
                for k in {d, nz - d}:
                    self.az[0, k] = term[x, at_z(k), :, self.ca].astype(BF16)
                    self.hz.append((k, links.send(self.az.at[0, k], self.az.at[1, k], dev_z(k))))

        def finish(self):
            value_b = term[x, z, :, self.cb]
            for k, handle in self.hx:
                links.arrived(handle, self.bx.at[1, k])
                value_b = value_b + self.bx[1, k].astype(F32)
            value_a = term[x, z, :, self.ca]
            for k, handle in self.hz:
                links.arrived(handle, self.az.at[1, k])
                value_a = value_a + self.az[1, k].astype(F32)
            return value_a, value_b

    sum_e = WeightSum(EARLY_A, EARLY_B, ax_e, az_e, bz_e, bx_e)
    sum_l = WeightSum(LATE_A, LATE_B, ax_l, az_l, bz_l, bx_l)

    def out_block(k):
        block = wg[at_y(k), :, :, :, WO : WO + 256].reshape(share, 256)
        for half in range(2):
            oterm[k, rows_of(half), :] = nt(gated[rows_of(half), :], block)

    ring_o = RingSum(
        links, lambda k, half: oterm[k, rows_of(half), :], yo_out, yo_in, dev_y(1), dev_y(3)
    )
    out_block(2)
    ring_o.start_far()
    sum_e.multiply(dt, gated[...], WO)
    sum_e.multiply(xt, gh[:, 0:256], GATE)
    out_block(1)
    ring_o.start_right()
    out_block(3)
    ring_o.start_left()
    out_block(0)
    sum_e.join()
    sum_e.start()

    def backward(head):
        for i in range(blocks):
            rows, cols = band(i)
            grad_weight = nt(ga[rows, head_cols(head)], part_of(act, VALUE, head, cols))
            grad_score = (grad_weight * sslope[head, rows, cols]).astype(BF16)
            sgrad[head, rows, cols] = grad_score
            grad_q = SCALE * nn(grad_score, part_of(act, KEY, head, cols))
            first = QUERY - GATE + head * DH
            gh[rows, first : first + DH] = (grad_q * part_of(slope, QUERY, head, rows)).astype(BF16)
        for j in range(blocks):
            cols = slice(j * 128, (j + 1) * 128)
            rows = slice(j * 128, min(j + 3, blocks) * 128)
            grad_k = SCALE * tn(sgrad[head, rows, cols], part_of(act, QUERY, head, rows))
            grad_v = tn(weights[head, rows, cols], ga[rows, head_cols(head)])
            for base, value in ((KEY, grad_k), (VALUE, grad_v)):
                first = base - GATE + head * DH
                gh[cols, first : first + DH] = (value * part_of(slope, base, head, cols)).astype(BF16)

    backward(0)
    sum_e.step_b()
    sum_e.middle_a()
    ring_o.middle()
    backward(1)
    sum_e.step_b()
    sum_l.multiply(xt, gh[:, 256:512], QUERY)
    sum_l.multiply(xt, gh[:, 512:768], KEY)
    sum_l.multiply(xt, gh[:, 768:1024], VALUE)
    sum_e.step_b()

    def in_block(k):
        block = wg[at_y(k), :, :, :, GATE:COLS].reshape(share, COLS - GATE)
        for half in range(2):
            iterm[k, rows_of(half), :] = nt(gh[rows_of(half), :], block)

    ring_i = RingSum(
        links, lambda k, half: iterm[k, rows_of(half), :], yi_out, yi_in, dev_y(1), dev_y(3)
    )
    in_block(2)
    ring_i.start_far()
    sum_l.join()
    sum_l.start()
    in_block(1)
    ring_i.start_right()
    in_block(3)
    ring_i.start_left()
    in_block(0)
    sum_e.turn_b()
    sum_e.turn_a()

    w_sum = jnp.zeros((1, COLS - GATE), F32)
    for k in range(NX):
        block = wg[k, :, :, :, GATE:COLS].reshape(share, COLS - GATE).astype(F32)
        w_sum = w_sum + jnp.sum(block, 0, keepdims=True)
    plain, cross = 0.0, 0.0
    for k in range((COLS - GATE) // 128):
        cols = slice(k * 128, (k + 1) * 128)
        piece = gh[:, cols].astype(F32)
        plain = plain + piece * w_sum[:, cols]
        cross = cross + piece * hid[:, cols]
    st2_own[0:1, :] = columns_sum(plain)
    st2_own[1:2, :] = columns_sum(cross)
    stat2 = [(k, links.send(st2_own, st2_in.at[y], dev_y(k))) for k in (1, 3, 2)]
    ring_i.middle()
    sum_l.step_b()
    sum_l.middle_a()

    for half, value in enumerate(ring_o.finish()):
        rows = rows_of(half)
        output[rows, :] = (xg[y, rows, :].astype(F32) + value).astype(BF16)
    sum_l.step_b()
    for k, handle in stat2:
        links.arrived(handle, st2_in.at[at_y(NY - k)])
    st2_in[y] = st2_own[...]
    sums2 = (st2_in[0] + st2_in[1] + st2_in[2] + st2_in[3]) / width
    row_avg, cross_avg = spread(sums2[0:1]), spread(sums2[1:2])
    sum_l.step_b()
    sum_l.turn_a()
    sum_l.turn_b()
    for half, value in enumerate(ring_i.finish()):
        rows = rows_of(half)
        here = slice(half * half_tok, (half + 1) * half_tok)
        for first in range(0, share, 128):
            cols = slice(first, min(first + 128, share))
            lanes = slice(0, cols.stop - cols.start)
            mean, inverse = row_stat[0, rows, lanes], row_stat[1, rows, lanes]
            normed = (xg[y, rows, cols].astype(F32) - mean) * inverse
            centred = value[:, cols] - row_avg[here, lanes] - normed * cross_avg[here, lanes]
            grad_input[rows, cols] = dg[y, rows, cols].astype(F32) + centred * inverse

    wo_part, gate_part = sum_e.finish()
    wo_back[...] = jnp.zeros(wo_back.shape, F32)
    wo_back[0:16, :] = wo_part
    grad_w_out[...] = wo_back[...].T[:, 0:16]
    low, high = sum_l.finish()
    pieces = {
        GATE: gate_part[:, 0:128],
        GATE + DH: gate_part[:, 128:256],
        QUERY: low[:, 0:128],
        QUERY + DH: low[:, 128:256],
        KEY: low[:, 256:384],
        KEY + DH: high[:, 0:128],
        VALUE: high[:, 128:256],
        VALUE + DH: high[:, 256:384],
    }
    for head in range(2):
        for part, base in enumerate((GATE, VALUE, QUERY, KEY)):
            target = head * 4 * DH + part * DH
            grad_w_in[:, target : target + DH] = pieces[base + head * DH]
    links.drain()


def shards(nz, history, out_grad, lengths, w_in, w_out):
    tok, share = history.shape
    width = share * NY
    half = tok // 2
    cols = COLS - GATE
    vmem = pltpu.VMEM
    weight_bufs = []
    for a, b in ((EARLY_A, EARLY_B), (LATE_A, LATE_B)):
        wa, wb = a[1] - a[0], b[1] - b[0]
        weight_bufs += [
            vmem((2, 6, nz // 2, 16, wa), BF16),
            vmem((2, nz, 16, wa), BF16),
            vmem((2, nz - 1, NX, 16, wb), BF16),
            vmem((2, NX, 16, wb), BF16),
        ]
    whole = pl.BlockSpec(memory_space=pltpu.VMEM)
    return pl.pallas_call(
        functools.partial(kernel, nz),
        out_shape=(
            jax.ShapeDtypeStruct((tok, share), BF16),
            jax.ShapeDtypeStruct((tok, share), F32),
            jax.ShapeDtypeStruct(w_in.shape, F32),
            jax.ShapeDtypeStruct(w_out.shape, F32),
        ),
        in_specs=[
            pl.BlockSpec(memory_space=pl.ANY),
            pl.BlockSpec(memory_space=pl.ANY),
            pl.BlockSpec(memory_space=pltpu.SMEM),
            whole,
            whole,
        ],
        out_specs=[whole] * 4,
        scratch_shapes=[
            vmem((NY, tok, share), BF16),
            vmem((NY, tok, share), BF16),
            vmem((tok, width), BF16),
            vmem((NX, nz, 2, 16, tok), BF16),
            vmem((NX, nz, 2, 16, tok), BF16),
            vmem((NX, nz, 2, 16, COLS), BF16),
            vmem((tok, cols), F32),
            vmem((tok, cols), F32),
            vmem((tok, cols), BF16),
            vmem((tok, tok), F32),
            vmem((2, tok, tok), BF16),
            vmem((2, tok, tok), F32),
            vmem((tok, 2 * DH), F32),
            vmem((tok, 2 * DH), F32),
            vmem((tok, 2 * DH), BF16),
            vmem((tok, 2 * DH), BF16),
            vmem((tok, cols), BF16),
            vmem((2, tok, tok), BF16),
            vmem((NX, nz, 16, COLS), F32),
            vmem((NX, nz, 16, COLS), BF16),
            vmem((NX, nz, 16, COLS), BF16),
            vmem((NY, tok, share), F32),
            vmem((NY, tok, share), F32),
            vmem((2, tok, 128), F32),
            vmem((8, tok), F32),
            vmem((NY, 8, tok), F32),
            vmem((8, tok), F32),
            vmem((NY, 8, tok), F32),
            vmem((6, half, share), BF16),
            vmem((6, half, share), BF16),
            vmem((6, half, share), BF16),
            vmem((6, half, share), BF16),
            vmem((2 * DH, 128), F32),
            vmem((128, 2 * DH), F32),
            *weight_bufs,
            pltpu.SemaphoreType.DMA((N_SEM,)),
            pltpu.SemaphoreType.DMA((N_SEM,)),
            pltpu.SemaphoreType.DMA((2,)),
        ],
        compiler_params=pltpu.CompilerParams(
            collective_id=0, has_side_effects=True, vmem_limit_bytes=60 * 1024 * 1024
        ),
    )(history, out_grad, lengths, w_in, w_out)


def solution(mesh):
    nz = mesh.shape["dp"] // (2 * NX)
    in_specs = (
        P("dp", "inner"),
        P("dp", "inner"),
        P("dp", None),
        P("dp", "inner"),
        P("inner", "dp"),
    )
    out_specs = (P("dp", "inner"), P("dp", "inner"), P("dp", "inner"), P("inner", "dp"))
    return jax.shard_map(
        functools.partial(shards, nz), mesh=mesh, in_specs=in_specs, out_specs=out_specs, check_vma=False
    )
```

```python
import functools

import jax
import jax.numpy as jnp
from jax import lax
from jax.experimental import pallas as pl
from jax.experimental.pallas import tpu as pltpu
from jax.sharding import PartitionSpec as P

H = 8
DH = 128
MAXLEN = 256
EPSILON = 1e-06
SCALE = DH ** (-0.5)
F32 = jnp.float32
BF16 = jnp.bfloat16
NX = 4
NY = 4
N_SEM = 64

HEAD = 3 * DH
QUERY, KEY, VALUE = 0, DH, 2 * DH
GATE, WO, COLS = 768, 1024, 1280
Z_ORDER = (4, 3, 5, 2, 6, 1, 7)


def nn(a, b):
    return lax.dot_general(a, b, (((1,), (0,)), ((), ())), preferred_element_type=F32)


def nt(a, b):
    return lax.dot_general(a, b, (((1,), (1,)), ((), ())), preferred_element_type=F32)


def tn(a, b):
    return lax.dot_general(a, b, (((0,), (0,)), ((), ())), preferred_element_type=F32)


class Links:
    def __init__(self, send_sem, recv_sem):
        self.send_sem, self.recv_sem, self.phases = send_sem, recv_sem, []

    def phase(self, region):
        return Phase(self, region)

    def drain(self):
        for phase in self.phases:
            phase.sent()


class Phase:
    def __init__(self, links, region):
        index = len(links.phases)
        assert index < N_SEM
        links.phases.append(self)
        self.sems = dict(send_sem=links.send_sem.at[index], recv_sem=links.recv_sem.at[index])
        self.region = region

    def copy(self, source, target, device):
        return pltpu.make_async_remote_copy(
            src_ref=source,
            dst_ref=target,
            device_id=device,
            device_id_type=pl.DeviceIdType.MESH,
            **self.sems,
        )

    def send(self, source, target, device):
        self.device = device
        self.copy(source, target, device).start()

    def arrived(self):
        self.copy(self.region, self.region, self.device).wait_recv()

    def sent(self):
        self.copy(self.region, self.region, self.device).wait_send()


class RingGather:
    def __init__(self, links, view, right, left, source, both):
        self.links, self.view, self.right, self.left = links, view, right, left
        self.source, self.both = source, both

    def start(self):
        view, source, links = self.view, self.source, self.links
        self.r0, self.l1 = links.phase(view(0, 0)), links.phase(view(0, 1))
        self.second = links.phase(self.both)
        self.r0.send(source(0), view(0, 0), self.right)
        self.l1.send(source(1), view(0, 1), self.left)
        self.second.send(source(1), view(0, 1), self.right)
        self.second.send(source(0), view(0, 0), self.left)

    def forward(self):
        view = self.view
        self.last = self.links.phase(self.both)
        self.r0.arrived()
        self.last.send(view(3, 0), view(3, 0), self.right)
        self.l1.arrived()
        self.last.send(view(1, 1), view(1, 1), self.left)

    def finish(self):
        self.second.arrived()
        self.last.arrived()


class RingSum:
    def __init__(self, links, part, out_buf, in_buf, right, left):
        self.links, self.part, self.out, self.inn = links, part, out_buf, in_buf
        self.right, self.left = right, left

    def push(self, phase, slot, value, device):
        self.out[slot] = value.astype(BF16)
        phase.send(self.out.at[slot], self.inn.at[slot], device)

    def start_far(self):
        links = self.links
        self.p0, self.p1 = links.phase(self.out.at[0]), links.phase(self.out.at[1])
        self.rest = links.phase(self.out.at[2:6])
        self.push(self.p0, 0, self.part(2, 0), self.right)
        self.push(self.p1, 1, self.part(2, 1), self.left)

    def start_right(self):
        self.push(self.rest, 2, self.part(1, 1), self.right)

    def start_left(self):
        self.push(self.rest, 3, self.part(3, 0), self.left)

    def middle(self):
        self.p0.arrived()
        self.push(self.rest, 4, self.inn[0].astype(F32) + self.part(1, 0), self.right)
        self.p1.arrived()
        self.push(self.rest, 5, self.inn[1].astype(F32) + self.part(3, 1), self.left)

    def finish(self):
        self.rest.arrived()
        first = self.part(0, 0) + self.inn[4].astype(F32) + self.inn[3].astype(F32)
        second = self.part(0, 1) + self.inn[2].astype(F32) + self.inn[5].astype(F32)
        return first, second


def kernel(
    nz,
    history,
    out_grad,
    lengths,
    w_in,
    w_out,
    output,
    grad_input,
    grad_w_in,
    grad_w_out,
    xg,
    dg,
    xh,
    xt,
    dt,
    wg,
    hid,
    slope,
    act,
    mask,
    weights,
    sslope,
    att,
    gg,
    ga,
    gated,
    gh,
    sgrad,
    term,
    sib_out,
    sib_in,
    oterm,
    iterm,
    row_stat,
    st_own,
    st_in,
    st2_own,
    st2_in,
    yo_out,
    yo_in,
    yi_out,
    yi_in,
    wsum,
    bufs_e,
    bufs_0,
    bufs_1,
    send_sem,
    recv_sem,
    local_sem,
):
    tok, share = history.shape
    half_tok = tok // 2
    width = share * NY
    me = lax.axis_index("dp")
    y = lax.axis_index("inner")
    core = lax.rem(me, 2)
    z = lax.rem(lax.div(me, 2), nz)
    x = lax.div(me, 2 * nz)
    other = 1 - core

    def at_x(k):
        return lax.rem(x + k, NX)

    def at_z(k):
        return lax.rem(z + k, nz)

    def at_y(k):
        return lax.rem(y + k, NY)

    def dev_x(k):
        return {"dp": (at_x(k) * nz + z) * 2 + core}

    def dev_z(k):
        return {"dp": (x * nz + at_z(k)) * 2 + core}

    def dev_y(k):
        return {"inner": at_y(k)}

    sibling = {"dp": (x * nz + z) * 2 + other}
    links = Links(send_sem, recv_sem)

    barrier = pltpu.get_barrier_semaphore()
    partners = (
        [sibling]
        + [dev_y(k) for k in (1, 2, 3)]
        + [dev_x(k) for k in (1, 2, 3)]
        + [dev_z(k) for k in range(1, nz)]
    )
    for device in partners:
        pl.semaphore_signal(barrier, inc=1, device_id=device, device_id_type=pl.DeviceIdType.MESH)

    own_x = pltpu.make_async_copy(history, xg.at[y], local_sem.at[0])
    own_d = pltpu.make_async_copy(out_grad, dg.at[y], local_sem.at[1])
    own_x.start()
    own_d.start()
    mine = (x, z, core, slice(None))
    wg[mine + (slice(WO, COLS),)] = w_out[...]
    for head in range(2):
        places = (GATE + head * DH, head * HEAD + VALUE, head * HEAD + QUERY, head * HEAD + KEY)
        for part, target in enumerate(places):
            source = (head * 4 + part) * DH
            wg[mine + (slice(target, target + DH),)] = w_in[:, source : source + DH]
    pl.semaphore_wait(barrier, len(partners))

    def rows_of(half):
        return pl.ds(half * half_tok, half_tok)

    gather_x = RingGather(
        links,
        lambda k, half: xg.at[at_y(k), rows_of(half)],
        dev_y(1),
        dev_y(3),
        lambda half: history.at[rows_of(half)],
        xg.at[0],
    )
    gather_d = RingGather(
        links,
        lambda k, half: dg.at[at_y(k), rows_of(half)],
        dev_y(1),
        dev_y(3),
        lambda half: out_grad.at[rows_of(half)],
        dg.at[0],
    )
    z_order = [k for k in Z_ORDER if k < nz] if nz == 8 else list(range(1, nz))
    x_order = (2, 1, 3)

    class WeightGather:
        def __init__(self, first, middle, end):
            self.ca = pl.ds(first, middle - first)
            self.cb = pl.ds(middle, end - middle) if end > middle else None

        def start(self):
            if self.cb:
                own = wg.at[x, z, core, :, self.cb]
                self.bx = links.phase(wg.at[0 : NX - 1, z, core, :, self.cb])
                for k in x_order:
                    self.bx.send(own, own, dev_x(k))
            own = wg.at[x, z, core, :, self.ca]
            self.az = links.phase(wg.at[x, 0 : nz - 1, core, :, self.ca])
            for k in z_order:
                self.az.send(own, own, dev_z(k))

        def turn_b(self):
            if self.cb:
                self.bx.arrived()
                slab = wg.at[:, z, core, :, self.cb]
                self.bz = links.phase(wg.at[:, 0 : nz - 1, core, :, self.cb])
                for k in z_order:
                    self.bz.send(slab, slab, dev_z(k))

        def turn_a(self):
            self.az.arrived()
            slab = wg.at[x, :, core, :, self.ca]
            self.ax = links.phase(wg.at[0 : NX - 1, :, core, :, self.ca])
            for k in x_order:
                self.ax.send(slab, slab, dev_x(k))

        def share(self):
            self.shared = []
            for last, cols in ((self.bz if self.cb else None, self.cb), (self.ax, self.ca)):
                if cols is not None:
                    last.arrived()
                    region = wg.at[:, :, core, :, cols]
                    phase = links.phase(region)
                    phase.send(region, region, sibling)
                    self.shared.append(phase)

        def finish(self):
            for phase in self.shared:
                phase.arrived()

    group_0 = WeightGather(0, 256, HEAD)
    group_1 = WeightGather(HEAD, HEAD + 256, 2 * HEAD)
    group_g = WeightGather(GATE, COLS, COLS)
    group_0.start()
    gather_x.start()
    group_1.start()
    group_g.start()

    blocks = tok // 128
    ends = []
    total = jnp.int32(0)
    for k in range(8):
        total = total + lengths[0, k]
        ends.append(total)
    for i in range(blocks):
        row = lax.broadcasted_iota(jnp.int32, (128, 128), 0) + i * 128
        begin = jnp.zeros((128, 128), jnp.int32)
        for k in range(7):
            begin = jnp.where(row >= ends[k], ends[k], begin)
        for j in range(max(0, i - 2), i + 1):
            col = lax.broadcasted_iota(jnp.int32, (128, 128), 1) + j * 128
            allowed = (col >= begin) & (col <= row)
            mask[i * 128 : (i + 1) * 128, j * 128 : (j + 1) * 128] = jnp.where(
                allowed, 1.0 / MAXLEN, 0.0
            ).astype(F32)

    group_0.turn_b()
    gather_x.forward()
    group_0.turn_a()
    group_1.turn_b()
    group_1.turn_a()
    group_g.turn_a()
    own_x.wait()
    gather_x.finish()
    gather_d.start()

    def norm_rows(block, carry):
        rows = pl.ds(pl.multiple_of(block * 128, 128), 128)
        cols = [xg[k, rows, :].astype(F32) for k in range(NY)]
        mean = sum(jnp.sum(part, 1, keepdims=True) for part in cols) / width
        square = sum(jnp.sum(part * part, 1, keepdims=True) for part in cols) / width
        inverse = lax.rsqrt(square - mean * mean + EPSILON)
        row_stat[0, rows, :] = jnp.broadcast_to(mean, (128, 128))
        row_stat[1, rows, :] = jnp.broadcast_to(inverse, (128, 128))
        for k in range(NY):
            xh[rows, k * share : (k + 1) * share] = ((cols[k] - mean) * inverse).astype(BF16)
        return carry

    lax.fori_loop(0, blocks, norm_rows, 0)
    group_0.share()

    def weight_cols(first, count):
        return wg[:, :, :, :, first : first + count].reshape(width, count)

    def hidden_cols(first, count):
        block = weight_cols(first, count)
        cols = slice(first, first + count)
        for half in range(2):
            rows = rows_of(half)
            value = nn(xh[rows, :], block)
            sigma = jax.nn.sigmoid(value)
            hid[rows, cols] = value
            act[rows, cols] = (value * sigma).astype(BF16)
            slope[rows, cols] = sigma * (1.0 + value * (1.0 - sigma))

    def cols_of(base, head):
        first = head * HEAD + base
        return slice(first, first + DH)

    def band(i):
        return slice(i * 128, (i + 1) * 128), slice(max(0, i - 2) * 128, (i + 1) * 128)

    def forward(head):
        for i in range(blocks):
            rows, cols = band(i)
            score = nt(act[rows, cols_of(QUERY, head)], act[cols, cols_of(KEY, head)]) * SCALE
            sigma = jax.nn.sigmoid(score)
            seen = mask[rows, cols]
            weight = (score * sigma * seen).astype(BF16)
            weights[head, rows, cols] = weight
            sslope[head, rows, cols] = sigma * (1.0 + score * (1.0 - sigma)) * seen
            att[rows, head * DH : (head + 1) * DH] = nn(weight, act[cols, cols_of(VALUE, head)])

    group_0.finish()
    hidden_cols(0, HEAD)
    gather_d.forward()
    group_1.share()
    forward(0)
    group_1.finish()
    hidden_cols(HEAD, HEAD)
    group_g.share()
    forward(1)
    own_d.wait()
    gather_d.finish()
    group_g.finish()
    hidden_cols(GATE, 2 * DH)
    for half in range(2):
        rows = rows_of(half)
        total_gg = None
        for k in range(NY):
            block = wg[k, :, :, :, WO:COLS].reshape(share, 2 * DH)
            piece = nn(dg[k, rows, :], block)
            total_gg = piece if total_gg is None else total_gg + piece
        gg[rows, :] = total_gg

    def columns_sum(value):
        return jnp.sum(value.T, 0, keepdims=True)

    def gate_of(head):
        return act[:, GATE + head * DH : GATE + (head + 1) * DH].astype(F32)

    def head_cols(head):
        return slice(head * DH, (head + 1) * DH)

    sums = [0.0] * 4
    for head in range(2):
        a = att[:, head_cols(head)]
        g = gg[:, head_cols(head)] * gate_of(head)
        for k, term_k in enumerate((a, a * a, g, g * a)):
            sums[k] = sums[k] + term_k
    for k in range(4):
        st_own[k : k + 1, :] = columns_sum(sums[k])
    stat = links.phase(st_in.at[0 : NY - 1])
    for k in x_order:
        stat.send(st_own, st_in.at[y], dev_y(k))
    for k in range(NY):
        cols = slice(k * share, (k + 1) * share)
        xt[k] = xh[:, cols].T.reshape(nz, 2, 16, tok)
        dt[k] = dg[k].T.reshape(nz, 2, 16, tok)
    w_sum = jnp.zeros((1, WO), F32)
    for k in range(NX):
        block = wg[k, :, :, :, 0:WO].reshape(share, WO).astype(F32)
        w_sum = w_sum + jnp.sum(block, 0, keepdims=True)
    wsum[...] = w_sum
    stat.arrived()
    st_in[y] = st_own[...]
    sums = st_in[0] + st_in[1] + st_in[2] + st_in[3]

    def spread(row_values):
        return jnp.broadcast_to(row_values, (128, tok)).T

    att_mean = sums[0:1] / (H * DH)
    att_inv = lax.rsqrt(sums[1:2] / (H * DH) - att_mean * att_mean + EPSILON)
    norm_mean = sums[2:3] / (H * DH)
    cross_mean = (sums[3:4] - att_mean * sums[2:3]) * att_inv / (H * DH)
    att_mean, att_inv, norm_mean, cross_mean = (
        spread(value) for value in (att_mean, att_inv, norm_mean, cross_mean)
    )
    for head in range(2):
        cols = head_cols(head)
        att_norm = (att[:, cols] - att_mean) * att_inv
        gate = gate_of(head)
        gated[:, cols] = (att_norm * gate).astype(BF16)
        g = gg[:, cols]
        here = slice(GATE + head * DH, GATE + (head + 1) * DH)
        gh[:, here] = (g * att_norm * slope[:, here]).astype(BF16)
        ga[:, cols] = ((g * gate - norm_mean - att_norm * cross_mean) * att_inv).astype(BF16)

    class WeightSum:
        def __init__(self, first, middle, end, bufs):
            self.a, self.b = slice(first, middle), slice(middle, end)
            self.all = slice(first, end)
            self.ax, self.az = bufs[0], bufs[1]
            self.bz, self.bx = bufs[2:4] if end > middle else (None, None)

        def multiply(self, products):
            everything = (slice(None), slice(None), slice(None))
            view = everything + (self.all,)
            for parity, own in ((other, False), (core, True)):
                for lhs, rhs, first in products:
                    count = rhs.shape[1]
                    here = everything + (slice(first, first + count),)
                    rows = lhs[:, :, parity].reshape(width // 2, tok)
                    value = nn(rows, rhs).reshape(NX, nz, 16, count)
                    if own:
                        term[here] = value
                    else:
                        sib_out[here] = value.astype(BF16)
                if not own:
                    self.pair = links.phase(sib_in.at[view])
                    self.pair.send(sib_out.at[view], sib_in.at[view], sibling)

        def joined(self, place):
            return term[place] + sib_in[place].astype(F32)

        def join(self):
            self.pair.arrived()
            if self.bz is not None:
                self.pz = links.phase(self.bz.at[0])
                for k in z_order:
                    self.bz[0, k - 1] = self.joined((slice(None), at_z(k), slice(None), self.b)).astype(BF16)
                    self.pz.send(self.bz.at[0, k - 1], self.bz.at[1, k - 1], dev_z(k))
            self.px = links.phase(self.ax.at[0])
            for k in x_order:
                self.ax[0, k - 1] = self.joined((at_x(k), slice(None), slice(None), self.a)).astype(BF16)
                self.px.send(self.ax.at[0, k - 1], self.ax.at[1, k - 1], dev_x(k))

        def turn_b(self):
            if self.bz is None:
                return
            place = (slice(None), z, slice(None), self.b)
            value = self.joined(place)
            self.pz.arrived()
            for k in range(nz - 1):
                value = value + self.bz[1, k].astype(F32)
            term[place] = value
            self.pxb = links.phase(self.bx.at[0])
            for k in x_order:
                self.bx[0, k - 1] = term[at_x(k), z, :, self.b].astype(BF16)
                self.pxb.send(self.bx.at[0, k - 1], self.bx.at[1, k - 1], dev_x(k))

        def turn_a(self):
            place = (x, slice(None), slice(None), self.a)
            value = self.joined(place)
            self.px.arrived()
            for k in range(NX - 1):
                value = value + self.ax[1, k].astype(F32)
            term[place] = value
            self.pza = links.phase(self.az.at[0])
            for k in z_order:
                self.az[0, k - 1] = term[x, at_z(k), :, self.a].astype(BF16)
                self.pza.send(self.az.at[0, k - 1], self.az.at[1, k - 1], dev_z(k))

        def finish(self):
            value_a = term[x, z, :, self.a]
            self.pza.arrived()
            for k in range(nz - 1):
                value_a = value_a + self.az[1, k].astype(F32)
            if self.bz is None:
                return value_a, None
            value_b = term[x, z, :, self.b]
            self.pxb.arrived()
            for k in range(NX - 1):
                value_b = value_b + self.bx[1, k].astype(F32)
            return value_a, value_b

    sum_e = WeightSum(GATE, COLS, COLS, bufs_e)
    sum_0 = WeightSum(0, 256, HEAD, bufs_0)
    sum_1 = WeightSum(HEAD, HEAD + 256, 2 * HEAD, bufs_1)

    def out_block(k):
        block = wg[at_y(k), :, :, :, WO:COLS].reshape(share, 2 * DH)
        for half in range(2):
            oterm[k, rows_of(half), :] = nt(gated[rows_of(half), :], block)

    def backward(head):
        mine_cols = head_cols(head)
        for i in range(blocks):
            rows, cols = band(i)
            grad_weight = nt(ga[rows, mine_cols], act[cols, cols_of(VALUE, head)])
            grad_score = (grad_weight * sslope[head, rows, cols]).astype(BF16)
            sgrad[head, rows, cols] = grad_score
            grad_q = SCALE * nn(grad_score, act[cols, cols_of(KEY, head)])
            here = cols_of(QUERY, head)
            gh[rows, here] = (grad_q * slope[rows, here]).astype(BF16)
        for j in range(blocks):
            cols = slice(j * 128, (j + 1) * 128)
            rows = slice(j * 128, min(j + 3, blocks) * 128)
            grad_k = SCALE * tn(sgrad[head, rows, cols], act[rows, cols_of(QUERY, head)])
            grad_v = tn(weights[head, rows, cols], ga[rows, mine_cols])
            for base, value in ((KEY, grad_k), (VALUE, grad_v)):
                here = cols_of(base, head)
                gh[cols, here] = (value * slope[cols, here]).astype(BF16)

    def in_block(k):
        block = wg[at_y(k), :, :, :, 0:WO].reshape(share, WO)
        for half in range(2):
            iterm[k, rows_of(half), :] = nt(gh[rows_of(half), :], block)

    ring_o = RingSum(
        links, lambda k, half: oterm[k, rows_of(half), :], yo_out, yo_in, dev_y(1), dev_y(3)
    )
    ring_i = RingSum(
        links, lambda k, half: iterm[k, rows_of(half), :], yi_out, yi_in, dev_y(1), dev_y(3)
    )

    sum_e.multiply([(dt, gated[...], WO), (xt, gh[:, GATE:WO], GATE)])
    out_block(2)
    ring_o.start_far()
    out_block(1)
    ring_o.start_right()
    out_block(3)
    ring_o.start_left()
    out_block(0)
    sum_e.join()
    backward(0)
    sum_0.multiply([(xt, gh[:, 0:HEAD], 0)])
    ring_o.middle()
    sum_0.join()
    backward(1)
    sum_1.multiply([(xt, gh[:, HEAD : 2 * HEAD], HEAD)])
    in_block(2)
    ring_i.start_far()
    sum_1.join()
    in_block(1)
    ring_i.start_right()
    in_block(3)
    ring_i.start_left()
    in_block(0)
    sum_e.turn_a()

    plain, cross = 0.0, 0.0
    for k in range(WO // 128):
        cols = slice(k * 128, (k + 1) * 128)
        piece = gh[:, cols].astype(F32)
        plain = plain + piece * wsum[:, cols]
        cross = cross + piece * hid[:, cols]
    st2_own[0:1, :] = columns_sum(plain)
    st2_own[1:2, :] = columns_sum(cross)
    stat2 = links.phase(st2_in.at[0 : NY - 1])
    for k in x_order:
        stat2.send(st2_own, st2_in.at[y], dev_y(k))
    sum_0.turn_b()
    sum_0.turn_a()
    ring_i.middle()
    for half, value in enumerate(ring_o.finish()):
        rows = rows_of(half)
        output[rows, :] = (xg[y, rows, :].astype(F32) + value).astype(BF16)
    sum_1.turn_b()
    sum_1.turn_a()
    stat2.arrived()
    st2_in[y] = st2_own[...]
    sums2 = (st2_in[0] + st2_in[1] + st2_in[2] + st2_in[3]) / width
    row_avg, cross_avg = spread(sums2[0:1]), spread(sums2[1:2])
    gate_part, _ = sum_e.finish()
    grad_w_out[...] = gate_part[:, 256:512]
    pieces = {GATE: gate_part[:, 0:128], GATE + DH: gate_part[:, 128:256]}
    for half, value in enumerate(ring_i.finish()):
        rows = rows_of(half)
        here = slice(half * half_tok, (half + 1) * half_tok)
        for first in range(0, share, 128):
            cols = slice(first, min(first + 128, share))
            lanes = slice(0, cols.stop - cols.start)
            mean, inverse = row_stat[0, rows, lanes], row_stat[1, rows, lanes]
            normed = (xg[y, rows, cols].astype(F32) - mean) * inverse
            centred = value[:, cols] - row_avg[here, lanes] - normed * cross_avg[here, lanes]
            grad_input[rows, cols] = dg[y, rows, cols].astype(F32) + centred * inverse
    for head, group in enumerate((sum_0, sum_1)):
        low, high = group.finish()
        pieces[head * HEAD + QUERY] = low[:, 0:128]
        pieces[head * HEAD + KEY] = low[:, 128:256]
        pieces[head * HEAD + VALUE] = high
    for head in range(2):
        places = (GATE + head * DH, head * HEAD + VALUE, head * HEAD + QUERY, head * HEAD + KEY)
        for part, place in enumerate(places):
            target = (head * 4 + part) * DH
            grad_w_in[:, target : target + DH] = pieces[place]
    links.drain()


def place_kernel(*refs):
    sems = refs[-1]
    count = len(refs) // 2
    copies = [
        pltpu.make_async_copy(refs[i], refs[count + i], sems.at[i]) for i in range(count)
    ]
    for copy in copies:
        copy.start()
    for copy in copies:
        copy.wait()


def shards(nz, history, out_grad, lengths, w_in, w_out):
    tok, share = history.shape
    width = share * NY
    half = tok // 2
    cols = WO
    vmem = pltpu.VMEM
    def sum_bufs(wa, wb):
        out = [vmem((2, NX - 1, nz, 16, wa), BF16), vmem((2, nz - 1, 16, wa), BF16)]
        if wb:
            out += [vmem((2, nz - 1, NX, 16, wb), BF16), vmem((2, NX - 1, 16, wb), BF16)]
        return out

    whole = pl.BlockSpec(memory_space=pltpu.VMEM)
    results = pl.pallas_call(
        functools.partial(kernel, nz),
        out_shape=(
            jax.ShapeDtypeStruct((tok, share), BF16),
            jax.ShapeDtypeStruct((tok, share), F32),
            jax.ShapeDtypeStruct(w_in.shape, F32),
            jax.ShapeDtypeStruct(w_out.shape[::-1], F32),
        ),
        in_specs=[
            pl.BlockSpec(memory_space=pl.ANY),
            pl.BlockSpec(memory_space=pl.ANY),
            pl.BlockSpec(memory_space=pltpu.SMEM),
            whole,
            whole,
        ],
        out_specs=[whole] * 4,
        scratch_shapes=[
            vmem((NY, tok, share), BF16),
            vmem((NY, tok, share), BF16),
            vmem((tok, width), BF16),
            vmem((NX, nz, 2, 16, tok), BF16),
            vmem((NX, nz, 2, 16, tok), BF16),
            vmem((NX, nz, 2, 16, COLS), BF16),
            vmem((tok, cols), F32),
            vmem((tok, cols), F32),
            vmem((tok, cols), BF16),
            vmem((tok, tok), F32),
            vmem((2, tok, tok), BF16),
            vmem((2, tok, tok), F32),
            vmem((tok, 2 * DH), F32),
            vmem((tok, 2 * DH), F32),
            vmem((tok, 2 * DH), BF16),
            vmem((tok, 2 * DH), BF16),
            vmem((tok, cols), BF16),
            vmem((2, tok, tok), BF16),
            vmem((NX, nz, 16, COLS), F32),
            vmem((NX, nz, 16, COLS), BF16),
            vmem((NX, nz, 16, COLS), BF16),
            vmem((NY, tok, share), F32),
            vmem((NY, tok, share), F32),
            vmem((2, tok, 128), F32),
            vmem((8, tok), F32),
            vmem((NY, 8, tok), F32),
            vmem((8, tok), F32),
            vmem((NY, 8, tok), F32),
            vmem((6, half, share), BF16),
            vmem((6, half, share), BF16),
            vmem((6, half, share), BF16),
            vmem((6, half, share), BF16),
            vmem((1, WO), F32),
            sum_bufs(512, 0),
            sum_bufs(256, 128),
            sum_bufs(256, 128),
            pltpu.SemaphoreType.DMA((N_SEM,)),
            pltpu.SemaphoreType.DMA((N_SEM,)),
            pltpu.SemaphoreType.DMA((2,)),
        ],
        compiler_params=pltpu.CompilerParams(
            collective_id=0, has_side_effects=True, vmem_limit_bytes=60 * 1024 * 1024
        ),
    )(history, out_grad, lengths, w_in, w_out.T)
    anywhere = pl.BlockSpec(memory_space=pl.ANY)
    output, grad_input, grad_w_in, grad_w_out = pl.pallas_call(
        place_kernel,
        out_shape=[jax.ShapeDtypeStruct(r.shape, r.dtype) for r in results],
        in_specs=[anywhere] * 4,
        out_specs=[anywhere] * 4,
        scratch_shapes=[pltpu.SemaphoreType.DMA((4,))],
    )(*results)
    return output, grad_input, grad_w_in, grad_w_out.T


def solution(mesh):
    nz = mesh.shape["dp"] // (2 * NX)
    in_specs = (
        P("dp", "inner"),
        P("dp", "inner"),
        P("dp", None),
        P("dp", "inner"),
        P("inner", "dp"),
    )
    out_specs = (P("dp", "inner"), P("dp", "inner"), P("dp", "inner"), P("inner", "dp"))
    return jax.shard_map(
        functools.partial(shards, nz), mesh=mesh, in_specs=in_specs, out_specs=out_specs, check_vma=False
    )
```

```python
import functools

import jax
import jax.numpy as jnp
from jax import lax
from jax.experimental import pallas as pl
from jax.experimental.pallas import tpu as pltpu
from jax.sharding import PartitionSpec as P

H = 8
DH = 128
MAXLEN = 256
EPSILON = 1e-06
SCALE = DH ** (-0.5)
F32 = jnp.float32
BF16 = jnp.bfloat16
NX = 4
NY = 4
N_SEM = 47

HEAD = 3 * DH
QUERY, KEY, VALUE = 0, DH, 2 * DH
GATE, WO, COLS = 768, 1024, 1280
Z_ORDER = (4, 3, 5, 2, 6, 1, 7)


def nn(a, b):
    return lax.dot_general(a, b, (((1,), (0,)), ((), ())), preferred_element_type=F32)


def nt(a, b):
    return lax.dot_general(a, b, (((1,), (1,)), ((), ())), preferred_element_type=F32)


def tn(a, b):
    return lax.dot_general(a, b, (((0,), (0,)), ((), ())), preferred_element_type=F32)


class Links:
    def __init__(self, send_sem, recv_sem):
        self.send_sem, self.recv_sem, self.phases = send_sem, recv_sem, []

    def phase(self, region):
        return Phase(self, region)

    def drain(self):
        for phase in self.phases:
            phase.sent()


class Phase:
    def __init__(self, links, region):
        index = len(links.phases)
        assert index < N_SEM
        links.phases.append(self)
        self.sems = dict(send_sem=links.send_sem.at[index], recv_sem=links.recv_sem.at[index])
        self.region = region

    def copy(self, source, target, device):
        return pltpu.make_async_remote_copy(
            src_ref=source,
            dst_ref=target,
            device_id=device,
            device_id_type=pl.DeviceIdType.MESH,
            **self.sems,
        )

    def send(self, source, target, device):
        self.device = device
        self.copy(source, target, device).start()

    def arrived(self):
        self.copy(self.region, self.region, self.device).wait_recv()

    def sent(self):
        self.copy(self.region, self.region, self.device).wait_send()


class RingGather:
    def __init__(self, links, view, right, left, source, both):
        self.links, self.view, self.right, self.left = links, view, right, left
        self.source, self.both = source, both

    def start(self):
        view, source, links = self.view, self.source, self.links
        self.r0, self.l1 = links.phase(view(0, 0)), links.phase(view(0, 1))
        self.second = links.phase(self.both)
        self.r0.send(source(0), view(0, 0), self.right)
        self.l1.send(source(1), view(0, 1), self.left)
        self.second.send(source(1), view(0, 1), self.right)
        self.second.send(source(0), view(0, 0), self.left)

    def forward(self):
        view = self.view
        self.last = self.links.phase(self.both)
        self.r0.arrived()
        self.last.send(view(3, 0), view(3, 0), self.right)
        self.l1.arrived()
        self.last.send(view(1, 1), view(1, 1), self.left)

    def finish(self):
        self.second.arrived()
        self.last.arrived()


class RingSum:
    def __init__(self, links, part, out_buf, in_buf, right, left):
        self.links, self.part, self.out, self.inn = links, part, out_buf, in_buf
        self.right, self.left = right, left

    def push(self, phase, slot, value, device):
        self.out[slot] = value.astype(BF16)
        phase.send(self.out.at[slot], self.inn.at[slot], device)

    def start_far(self):
        links = self.links
        self.p0, self.p1 = links.phase(self.out.at[0]), links.phase(self.out.at[1])
        self.rest = links.phase(self.out.at[2:6])
        self.push(self.p0, 0, self.part(2, 0), self.right)
        self.push(self.p1, 1, self.part(2, 1), self.left)

    def start_right(self):
        self.push(self.rest, 2, self.part(1, 1), self.right)

    def start_left(self):
        self.push(self.rest, 3, self.part(3, 0), self.left)

    def middle(self):
        self.p0.arrived()
        self.push(self.rest, 4, self.inn[0].astype(F32) + self.part(1, 0), self.right)
        self.p1.arrived()
        self.push(self.rest, 5, self.inn[1].astype(F32) + self.part(3, 1), self.left)

    def finish(self):
        self.rest.arrived()
        first = self.part(0, 0) + self.inn[4].astype(F32) + self.inn[3].astype(F32)
        second = self.part(0, 1) + self.inn[2].astype(F32) + self.inn[5].astype(F32)
        return first, second


def kernel(
    nz,
    history,
    out_grad,
    lengths,
    w_in,
    w_out,
    output_hbm,
    grad_input_hbm,
    grad_w_in_hbm,
    grad_w_out_hbm,
    output,
    grad_input,
    grad_w_in,
    grad_w_out,
    xg,
    dg,
    xh,
    xt,
    dt,
    wg,
    hid,
    slope,
    act,
    mask,
    weights,
    sslope,
    att,
    gg,
    ga,
    gated,
    gh,
    sgrad,
    term,
    sib_out,
    sib_in,
    oterm,
    iterm,
    row_stat,
    st_own,
    st_in,
    st2_own,
    st2_in,
    yo_out,
    yo_in,
    yi_out,
    yi_in,
    wsum,
    bufs_e,
    bufs_0,
    bufs_1,
    send_sem,
    recv_sem,
    local_sem,
):
    tok, share = history.shape
    half_tok = tok // 2
    width = share * NY
    me = lax.axis_index("dp")
    y = lax.axis_index("inner")
    core = lax.rem(me, 2)
    z = lax.rem(lax.div(me, 2), nz)
    x = lax.div(me, 2 * nz)
    other = 1 - core

    def at_x(k):
        return lax.rem(x + k, NX)

    def at_z(k):
        return lax.rem(z + k, nz)

    def at_y(k):
        return lax.rem(y + k, NY)

    def dev_x(k):
        return {"dp": (at_x(k) * nz + z) * 2 + core}

    def dev_z(k):
        return {"dp": (x * nz + at_z(k)) * 2 + core}

    def dev_y(k):
        return {"inner": at_y(k)}

    sibling = {"dp": (x * nz + z) * 2 + other}
    links = Links(send_sem, recv_sem)

    written = []

    def write(index, source, target):
        copy = pltpu.make_async_copy(source, target, local_sem.at[2 + index])
        copy.start()
        written.append(copy)

    barrier = pltpu.get_barrier_semaphore()
    partners = (
        [sibling]
        + [dev_y(k) for k in (1, 2, 3)]
        + [dev_x(k) for k in (1, 2, 3)]
        + [dev_z(k) for k in range(1, nz)]
    )
    for device in partners:
        pl.semaphore_signal(barrier, inc=1, device_id=device, device_id_type=pl.DeviceIdType.MESH)

    own_x = pltpu.make_async_copy(history, xg.at[y], local_sem.at[0])
    own_d = pltpu.make_async_copy(out_grad, dg.at[y], local_sem.at[1])
    own_x.start()
    own_d.start()
    mine = (x, z, core, slice(None))
    wg[mine + (slice(WO, COLS),)] = w_out[...]
    for head in range(2):
        places = (GATE + head * DH, head * HEAD + VALUE, head * HEAD + QUERY, head * HEAD + KEY)
        for part, target in enumerate(places):
            source = (head * 4 + part) * DH
            wg[mine + (slice(target, target + DH),)] = w_in[:, source : source + DH]
    pl.semaphore_wait(barrier, len(partners))

    def rows_of(half):
        return pl.ds(half * half_tok, half_tok)

    gather_x = RingGather(
        links,
        lambda k, half: xg.at[at_y(k), rows_of(half)],
        dev_y(1),
        dev_y(3),
        lambda half: history.at[rows_of(half)],
        xg.at[0],
    )
    gather_d = RingGather(
        links,
        lambda k, half: dg.at[at_y(k), rows_of(half)],
        dev_y(1),
        dev_y(3),
        lambda half: out_grad.at[rows_of(half)],
        dg.at[0],
    )
    z_order = [k for k in Z_ORDER if k < nz] if nz == 8 else list(range(1, nz))
    x_order = (2, 1, 3)

    class WeightGather:
        def __init__(self, first, middle, end):
            self.ca = pl.ds(first, middle - first)
            self.cb = pl.ds(middle, end - middle) if end > middle else None

        def start(self):
            if self.cb:
                own = wg.at[x, z, core, :, self.cb]
                self.bx = links.phase(wg.at[0 : NX - 1, z, core, :, self.cb])
                for k in x_order:
                    self.bx.send(own, own, dev_x(k))
            own = wg.at[x, z, core, :, self.ca]
            self.az = links.phase(wg.at[x, 0 : nz - 1, core, :, self.ca])
            for k in z_order:
                self.az.send(own, own, dev_z(k))

        def turn_b(self):
            if self.cb:
                self.bx.arrived()
                slab = wg.at[:, z, core, :, self.cb]
                self.bz = links.phase(wg.at[:, 0 : nz - 1, core, :, self.cb])
                for k in z_order:
                    self.bz.send(slab, slab, dev_z(k))

        def turn_a(self):
            self.az.arrived()
            slab = wg.at[x, :, core, :, self.ca]
            self.ax = links.phase(wg.at[0 : NX - 1, :, core, :, self.ca])
            for k in x_order:
                self.ax.send(slab, slab, dev_x(k))

        def share(self):
            self.shared = []
            for last, cols in ((self.bz if self.cb else None, self.cb), (self.ax, self.ca)):
                if cols is not None:
                    last.arrived()
                    region = wg.at[:, :, core, :, cols]
                    phase = links.phase(region)
                    phase.send(region, region, sibling)
                    self.shared.append(phase)

        def finish(self):
            for phase in self.shared:
                phase.arrived()

    group_0 = WeightGather(0, 256, HEAD)
    group_1 = WeightGather(HEAD, HEAD + 256, 2 * HEAD)
    group_g = WeightGather(GATE, GATE + 384, COLS)
    group_0.start()
    gather_x.start()
    group_1.start()
    group_g.start()

    blocks = tok // 128
    ends = []
    total = jnp.int32(0)
    for k in range(8):
        total = total + lengths[0, k]
        ends.append(total)
    for i in range(blocks):
        row = lax.broadcasted_iota(jnp.int32, (128, 128), 0) + i * 128
        begin = jnp.zeros((128, 128), jnp.int32)
        for k in range(7):
            begin = jnp.where(row >= ends[k], ends[k], begin)
        for j in range(max(0, i - 2), i + 1):
            col = lax.broadcasted_iota(jnp.int32, (128, 128), 1) + j * 128
            allowed = (col >= begin) & (col <= row)
            mask[i * 128 : (i + 1) * 128, j * 128 : (j + 1) * 128] = jnp.where(
                allowed, 1.0 / MAXLEN, 0.0
            ).astype(F32)

    group_0.turn_b()
    gather_x.forward()
    gather_d.start()
    group_0.turn_a()
    group_1.turn_b()
    group_1.turn_a()
    group_g.turn_b()
    group_g.turn_a()
    own_x.wait()
    gather_x.finish()

    def norm_rows(block, carry):
        rows = pl.ds(pl.multiple_of(block * 128, 128), 128)
        cols = [xg[k, rows, :].astype(F32) for k in range(NY)]
        mean = sum(jnp.sum(part, 1, keepdims=True) for part in cols) / width
        square = sum(jnp.sum(part * part, 1, keepdims=True) for part in cols) / width
        inverse = lax.rsqrt(square - mean * mean + EPSILON)
        row_stat[0, rows, :] = jnp.broadcast_to(mean, (128, 128))
        row_stat[1, rows, :] = jnp.broadcast_to(inverse, (128, 128))
        for k in range(NY):
            xh[rows, k * share : (k + 1) * share] = ((cols[k] - mean) * inverse).astype(BF16)
        return carry

    lax.fori_loop(0, blocks, norm_rows, 0)
    group_0.share()

    def weight_cols(first, count):
        return wg[:, :, :, :, first : first + count].reshape(width, count)

    def hidden_cols(first, count):
        block = weight_cols(first, count)
        cols = slice(first, first + count)
        for half in range(2):
            rows = rows_of(half)
            value = nn(xh[rows, :], block)
            sigma = jax.nn.sigmoid(value)
            hid[rows, cols] = value
            act[rows, cols] = (value * sigma).astype(BF16)
            slope[rows, cols] = sigma * (1.0 + value * (1.0 - sigma))

    def cols_of(base, head):
        first = head * HEAD + base
        return slice(first, first + DH)

    def band(i):
        return slice(i * 128, (i + 1) * 128), slice(max(0, i - 2) * 128, (i + 1) * 128)

    def forward(head):
        for i in range(blocks):
            rows, cols = band(i)
            score = nt(act[rows, cols_of(QUERY, head)], act[cols, cols_of(KEY, head)]) * SCALE
            sigma = jax.nn.sigmoid(score)
            seen = mask[rows, cols]
            weight = (score * sigma * seen).astype(BF16)
            weights[head, rows, cols] = weight
            sslope[head, rows, cols] = sigma * (1.0 + score * (1.0 - sigma)) * seen
            att[rows, head * DH : (head + 1) * DH] = nn(weight, act[cols, cols_of(VALUE, head)])

    group_0.finish()
    gather_d.forward()
    hidden_cols(0, HEAD)
    group_1.share()
    forward(0)
    group_1.finish()
    hidden_cols(HEAD, HEAD)
    group_g.share()
    forward(1)
    own_d.wait()
    gather_d.finish()
    group_g.finish()
    hidden_cols(GATE, 2 * DH)
    for half in range(2):
        rows = rows_of(half)
        total_gg = None
        for k in range(NY):
            block = wg[k, :, :, :, WO:COLS].reshape(share, 2 * DH)
            piece = nn(dg[k, rows, :], block)
            total_gg = piece if total_gg is None else total_gg + piece
        gg[rows, :] = total_gg

    def columns_sum(value):
        return jnp.sum(value.T, 0, keepdims=True)

    def gate_of(head):
        return act[:, GATE + head * DH : GATE + (head + 1) * DH].astype(F32)

    def head_cols(head):
        return slice(head * DH, (head + 1) * DH)

    sums = [0.0] * 4
    for head in range(2):
        a = att[:, head_cols(head)]
        g = gg[:, head_cols(head)] * gate_of(head)
        for k, term_k in enumerate((a, a * a, g, g * a)):
            sums[k] = sums[k] + term_k
    for k in range(4):
        st_own[k : k + 1, :] = columns_sum(sums[k])
    stat = links.phase(st_in.at[0 : NY - 1])
    for k in x_order:
        stat.send(st_own, st_in.at[y], dev_y(k))
    for k in range(NY):
        cols = slice(k * share, (k + 1) * share)
        xt[k] = xh[:, cols].T.reshape(nz, 2, 16, tok)
        dt[k] = dg[k].T.reshape(nz, 2, 16, tok)
    w_sum = jnp.zeros((1, WO), F32)
    for k in range(NX):
        block = wg[k, :, :, :, 0:WO].reshape(share, WO).astype(F32)
        w_sum = w_sum + jnp.sum(block, 0, keepdims=True)
    wsum[...] = w_sum
    stat.arrived()
    st_in[y] = st_own[...]
    sums = st_in[0] + st_in[1] + st_in[2] + st_in[3]

    def spread(row_values):
        return jnp.broadcast_to(row_values, (128, tok)).T

    att_mean = sums[0:1] / (H * DH)
    att_inv = lax.rsqrt(sums[1:2] / (H * DH) - att_mean * att_mean + EPSILON)
    norm_mean = sums[2:3] / (H * DH)
    cross_mean = (sums[3:4] - att_mean * sums[2:3]) * att_inv / (H * DH)
    att_mean, att_inv, norm_mean, cross_mean = (
        spread(value) for value in (att_mean, att_inv, norm_mean, cross_mean)
    )
    for head in range(2):
        cols = head_cols(head)
        gated[:, cols] = ((att[:, cols] - att_mean) * att_inv * gate_of(head)).astype(BF16)

    def out_block(k):
        block = wg[at_y(k), :, :, :, WO:COLS].reshape(share, 2 * DH)
        for half in range(2):
            oterm[k, rows_of(half), :] = nt(gated[rows_of(half), :], block)

    ring_o = RingSum(
        links, lambda k, half: oterm[k, rows_of(half), :], yo_out, yo_in, dev_y(1), dev_y(3)
    )
    out_block(2)
    ring_o.start_far()
    out_block(1)
    ring_o.start_right()
    out_block(3)
    ring_o.start_left()
    for head in range(2):
        cols = head_cols(head)
        att_norm = (att[:, cols] - att_mean) * att_inv
        gate = gate_of(head)
        g = gg[:, cols]
        here = slice(GATE + head * DH, GATE + (head + 1) * DH)
        gh[:, here] = (g * att_norm * slope[:, here]).astype(BF16)
        ga[:, cols] = ((g * gate - norm_mean - att_norm * cross_mean) * att_inv).astype(BF16)

    class WeightSum:
        def __init__(self, first, middle, end, bufs):
            self.a, self.b = slice(first, middle), slice(middle, end)
            self.all = slice(first, end)
            self.ax, self.az = bufs[0], bufs[1]
            self.bz, self.bx = bufs[2:4] if end > middle else (None, None)

        def multiply(self, products):
            everything = (slice(None), slice(None), slice(None))
            view = everything + (self.all,)
            for parity, own in ((other, False), (core, True)):
                for lhs, rhs, first in products:
                    count = rhs.shape[1]
                    here = everything + (slice(first, first + count),)
                    rows = lhs[:, :, parity].reshape(width // 2, tok)
                    value = nn(rows, rhs).reshape(NX, nz, 16, count)
                    if own:
                        term[here] = value
                    else:
                        sib_out[here] = value.astype(BF16)
                if not own:
                    self.pair = links.phase(sib_in.at[view])
                    self.pair.send(sib_out.at[view], sib_in.at[view], sibling)

        def joined(self, place):
            return term[place] + sib_in[place].astype(F32)

        def join(self):
            self.pair.arrived()
            if self.bz is not None:
                self.pz = links.phase(self.bz.at[0])
                for k in z_order:
                    self.bz[0, k - 1] = self.joined((slice(None), at_z(k), slice(None), self.b)).astype(BF16)
                    self.pz.send(self.bz.at[0, k - 1], self.bz.at[1, k - 1], dev_z(k))
            self.px = links.phase(self.ax.at[0])
            for k in x_order:
                self.ax[0, k - 1] = self.joined((at_x(k), slice(None), slice(None), self.a)).astype(BF16)
                self.px.send(self.ax.at[0, k - 1], self.ax.at[1, k - 1], dev_x(k))

        def turn_b(self):
            if self.bz is None:
                return
            place = (slice(None), z, slice(None), self.b)
            value = self.joined(place)
            self.pz.arrived()
            for k in range(nz - 1):
                value = value + self.bz[1, k].astype(F32)
            term[place] = value
            self.pxb = links.phase(self.bx.at[0])
            for k in x_order:
                self.bx[0, k - 1] = term[at_x(k), z, :, self.b].astype(BF16)
                self.pxb.send(self.bx.at[0, k - 1], self.bx.at[1, k - 1], dev_x(k))

        def turn_a(self):
            place = (x, slice(None), slice(None), self.a)
            value = self.joined(place)
            self.px.arrived()
            for k in range(NX - 1):
                value = value + self.ax[1, k].astype(F32)
            term[place] = value
            self.pza = links.phase(self.az.at[0])
            for k in z_order:
                self.az[0, k - 1] = term[x, at_z(k), :, self.a].astype(BF16)
                self.pza.send(self.az.at[0, k - 1], self.az.at[1, k - 1], dev_z(k))

        def finish(self):
            value_a = term[x, z, :, self.a]
            self.pza.arrived()
            for k in range(nz - 1):
                value_a = value_a + self.az[1, k].astype(F32)
            if self.bz is None:
                return value_a, None
            value_b = term[x, z, :, self.b]
            self.pxb.arrived()
            for k in range(NX - 1):
                value_b = value_b + self.bx[1, k].astype(F32)
            return value_a, value_b

    sum_e = WeightSum(GATE, COLS, COLS, bufs_e)
    sum_0 = WeightSum(0, 256, HEAD, bufs_0)
    sum_1 = WeightSum(HEAD, HEAD + 256, 2 * HEAD, bufs_1)

    def backward(head):
        mine_cols = head_cols(head)
        for i in range(blocks):
            rows, cols = band(i)
            grad_weight = nt(ga[rows, mine_cols], act[cols, cols_of(VALUE, head)])
            grad_score = (grad_weight * sslope[head, rows, cols]).astype(BF16)
            sgrad[head, rows, cols] = grad_score
            grad_q = SCALE * nn(grad_score, act[cols, cols_of(KEY, head)])
            here = cols_of(QUERY, head)
            gh[rows, here] = (grad_q * slope[rows, here]).astype(BF16)
        for j in range(blocks):
            cols = slice(j * 128, (j + 1) * 128)
            rows = slice(j * 128, min(j + 3, blocks) * 128)
            grad_k = SCALE * tn(sgrad[head, rows, cols], act[rows, cols_of(QUERY, head)])
            grad_v = tn(weights[head, rows, cols], ga[rows, mine_cols])
            for base, value in ((KEY, grad_k), (VALUE, grad_v)):
                here = cols_of(base, head)
                gh[cols, here] = (value * slope[cols, here]).astype(BF16)

    def in_block(k):
        block = wg[at_y(k), :, :, :, 0:WO].reshape(share, WO)
        for half in range(2):
            iterm[k, rows_of(half), :] = nt(gh[rows_of(half), :], block)

    ring_i = RingSum(
        links, lambda k, half: iterm[k, rows_of(half), :], yi_out, yi_in, dev_y(1), dev_y(3)
    )

    sum_e.multiply([(dt, gated[...], WO), (xt, gh[:, GATE:WO], GATE)])
    out_block(0)
    sum_e.join()
    backward(0)
    sum_0.multiply([(xt, gh[:, 0:HEAD], 0)])
    ring_o.middle()
    sum_0.join()
    backward(1)
    sum_1.multiply([(xt, gh[:, HEAD : 2 * HEAD], HEAD)])
    in_block(2)
    ring_i.start_far()
    sum_1.join()
    in_block(1)
    ring_i.start_right()
    in_block(3)
    ring_i.start_left()
    in_block(0)
    sum_e.turn_a()

    plain, cross = 0.0, 0.0
    for k in range(WO // 128):
        cols = slice(k * 128, (k + 1) * 128)
        piece = gh[:, cols].astype(F32)
        plain = plain + piece * wsum[:, cols]
        cross = cross + piece * hid[:, cols]
    st2_own[0:1, :] = columns_sum(plain)
    st2_own[1:2, :] = columns_sum(cross)
    stat2 = links.phase(st2_in.at[0 : NY - 1])
    for k in x_order:
        stat2.send(st2_own, st2_in.at[y], dev_y(k))
    sum_0.turn_b()
    sum_0.turn_a()
    ring_i.middle()
    for half, value in enumerate(ring_o.finish()):
        rows = rows_of(half)
        output[rows, :] = (xg[y, rows, :].astype(F32) + value).astype(BF16)
    write(0, output, output_hbm)
    sum_1.turn_b()
    sum_1.turn_a()
    stat2.arrived()
    st2_in[y] = st2_own[...]
    sums2 = (st2_in[0] + st2_in[1] + st2_in[2] + st2_in[3]) / width
    row_avg, cross_avg = spread(sums2[0:1]), spread(sums2[1:2])
    gate_part, _ = sum_e.finish()
    grad_w_out[...] = gate_part[:, 256:512]
    write(1, grad_w_out, grad_w_out_hbm)
    pieces = {GATE: gate_part[:, 0:128], GATE + DH: gate_part[:, 128:256]}
    for half, value in enumerate(ring_i.finish()):
        rows = rows_of(half)
        here = slice(half * half_tok, (half + 1) * half_tok)
        for first in range(0, share, 128):
            cols = slice(first, min(first + 128, share))
            lanes = slice(0, cols.stop - cols.start)
            mean, inverse = row_stat[0, rows, lanes], row_stat[1, rows, lanes]
            normed = (xg[y, rows, cols].astype(F32) - mean) * inverse
            centred = value[:, cols] - row_avg[here, lanes] - normed * cross_avg[here, lanes]
            grad_input[rows, cols] = dg[y, rows, cols].astype(F32) + centred * inverse
    write(2, grad_input, grad_input_hbm)
    for head, group in enumerate((sum_0, sum_1)):
        low, high = group.finish()
        pieces[head * HEAD + QUERY] = low[:, 0:128]
        pieces[head * HEAD + KEY] = low[:, 128:256]
        pieces[head * HEAD + VALUE] = high
    for head in range(2):
        places = (GATE + head * DH, head * HEAD + VALUE, head * HEAD + QUERY, head * HEAD + KEY)
        for part, place in enumerate(places):
            target = (head * 4 + part) * DH
            grad_w_in[:, target : target + DH] = pieces[place]
    write(3, grad_w_in, grad_w_in_hbm)
    links.drain()
    for copy in written:
        copy.wait()


def place_kernel(*refs):
    sources, targets, held, sems = refs[:4], refs[4:8], refs[8:12], refs[12]
    inward = [pltpu.make_async_copy(sources[i], held[i], sems.at[i]) for i in range(4)]
    outward = [pltpu.make_async_copy(held[i], targets[i], sems.at[4 + i]) for i in range(4)]
    for copy in inward:
        copy.start()
    for i in range(4):
        inward[i].wait()
        outward[i].start()
    for copy in outward:
        copy.wait()


def shards(nz, history, out_grad, lengths, w_in, w_out):
    tok, share = history.shape
    width = share * NY
    half = tok // 2
    cols = WO
    vmem = pltpu.VMEM
    def sum_bufs(wa, wb):
        out = [vmem((2, NX - 1, nz, 16, wa), BF16), vmem((2, nz - 1, 16, wa), BF16)]
        if wb:
            out += [vmem((2, nz - 1, NX, 16, wb), BF16), vmem((2, NX - 1, 16, wb), BF16)]
        return out

    whole = pl.BlockSpec(memory_space=pltpu.VMEM)
    results = pl.pallas_call(
        functools.partial(kernel, nz),
        out_shape=(
            jax.ShapeDtypeStruct((tok, share), BF16),
            jax.ShapeDtypeStruct((tok, share), F32),
            jax.ShapeDtypeStruct(w_in.shape, F32),
            jax.ShapeDtypeStruct(w_out.shape[::-1], F32),
        ),
        in_specs=[
            pl.BlockSpec(memory_space=pl.ANY),
            pl.BlockSpec(memory_space=pl.ANY),
            pl.BlockSpec(memory_space=pltpu.SMEM),
            whole,
            whole,
        ],
        out_specs=[pl.BlockSpec(memory_space=pl.ANY)] * 4,
        scratch_shapes=[
            vmem((tok, share), BF16),
            vmem((tok, share), F32),
            vmem(w_in.shape, F32),
            vmem(w_out.shape[::-1], F32),
            vmem((NY, tok, share), BF16),
            vmem((NY, tok, share), BF16),
            vmem((tok, width), BF16),
            vmem((NX, nz, 2, 16, tok), BF16),
            vmem((NX, nz, 2, 16, tok), BF16),
            vmem((NX, nz, 2, 16, COLS), BF16),
            vmem((tok, cols), F32),
            vmem((tok, cols), F32),
            vmem((tok, cols), BF16),
            vmem((tok, tok), F32),
            vmem((2, tok, tok), BF16),
            vmem((2, tok, tok), F32),
            vmem((tok, 2 * DH), F32),
            vmem((tok, 2 * DH), F32),
            vmem((tok, 2 * DH), BF16),
            vmem((tok, 2 * DH), BF16),
            vmem((tok, cols), BF16),
            vmem((2, tok, tok), BF16),
            vmem((NX, nz, 16, COLS), F32),
            vmem((NX, nz, 16, COLS), BF16),
            vmem((NX, nz, 16, COLS), BF16),
            vmem((NY, tok, share), F32),
            vmem((NY, tok, share), F32),
            vmem((2, tok, 128), F32),
            vmem((8, tok), F32),
            vmem((NY, 8, tok), F32),
            vmem((8, tok), F32),
            vmem((NY, 8, tok), F32),
            vmem((6, half, share), BF16),
            vmem((6, half, share), BF16),
            vmem((6, half, share), BF16),
            vmem((6, half, share), BF16),
            vmem((1, WO), F32),
            sum_bufs(512, 0),
            sum_bufs(256, 128),
            sum_bufs(256, 128),
            pltpu.SemaphoreType.DMA((N_SEM,)),
            pltpu.SemaphoreType.DMA((N_SEM,)),
            pltpu.SemaphoreType.DMA((6,)),
        ],
        compiler_params=pltpu.CompilerParams(
            collective_id=0, has_side_effects=True, vmem_limit_bytes=60 * 1024 * 1024
        ),
    )(history, out_grad, lengths, w_in, w_out.T)
    anywhere = pl.BlockSpec(memory_space=pl.ANY)
    output, grad_input, grad_w_in, grad_w_out = pl.pallas_call(
        place_kernel,
        out_shape=[jax.ShapeDtypeStruct(r.shape, r.dtype) for r in results],
        in_specs=[anywhere] * 4,
        out_specs=[anywhere] * 4,
        scratch_shapes=[vmem(r.shape, r.dtype) for r in results] + [pltpu.SemaphoreType.DMA((8,))],
    )(*results)
    return output, grad_input, grad_w_in, grad_w_out.T


def solution(mesh):
    nz = mesh.shape["dp"] // (2 * NX)
    in_specs = (
        P("dp", "inner"),
        P("dp", "inner"),
        P("dp", None),
        P("dp", "inner"),
        P("inner", "dp"),
    )
    out_specs = (P("dp", "inner"), P("dp", "inner"), P("dp", "inner"), P("inner", "dp"))
    return jax.shard_map(
        functools.partial(shards, nz), mesh=mesh, in_specs=in_specs, out_specs=out_specs, check_vma=False
    )
```

```python
import functools

import jax
import jax.numpy as jnp
from jax import lax
from jax.experimental import pallas as pl
from jax.experimental.pallas import tpu as pltpu
from jax.sharding import PartitionSpec as P

H = 8
DH = 128
MAXLEN = 256
EPSILON = 1e-06
SCALE = DH ** (-0.5)
F32 = jnp.float32
BF16 = jnp.bfloat16
NX = 4
NY = 4
N_SEM = 59

HEAD = 3 * DH
QUERY, KEY, VALUE = 0, DH, 2 * DH
GATE, WO, COLS = 768, 1024, 1280


def nn(a, b):
    return lax.dot_general(a, b, (((1,), (0,)), ((), ())), preferred_element_type=F32)


def nt(a, b):
    return lax.dot_general(a, b, (((1,), (1,)), ((), ())), preferred_element_type=F32)


def tn(a, b):
    return lax.dot_general(a, b, (((0,), (0,)), ((), ())), preferred_element_type=F32)


class Links:
    def __init__(self, send_sem, recv_sem):
        self.send_sem, self.recv_sem, self.phases, self.drained = send_sem, recv_sem, [], 0

    def phase(self, region):
        return Phase(self, region)

    def drain(self):
        for phase in self.phases[self.drained :]:
            phase.sent()
        self.drained = len(self.phases)


class Phase:
    def __init__(self, links, region):
        index = len(links.phases)
        assert index < N_SEM
        links.phases.append(self)
        self.sems = dict(send_sem=links.send_sem.at[index], recv_sem=links.recv_sem.at[index])
        self.region = region

    def copy(self, source, target, device):
        return pltpu.make_async_remote_copy(
            src_ref=source,
            dst_ref=target,
            device_id=device,
            device_id_type=pl.DeviceIdType.MESH,
            **self.sems,
        )

    def send(self, source, target, device):
        self.device = device
        self.copy(source, target, device).start()

    def arrived(self):
        self.copy(self.region, self.region, self.device).wait_recv()

    def sent(self):
        self.copy(self.region, self.region, self.device).wait_send()


class RingGather:
    def __init__(self, links, view, right, left, source, both):
        self.links, self.view, self.right, self.left = links, view, right, left
        self.source, self.both = source, both

    def start(self):
        view, source, links = self.view, self.source, self.links
        self.r0, self.l1 = links.phase(view(0, 0)), links.phase(view(0, 1))
        self.second = links.phase(self.both)
        self.r0.send(source(0), view(0, 0), self.right)
        self.l1.send(source(1), view(0, 1), self.left)
        self.second.send(source(1), view(0, 1), self.right)
        self.second.send(source(0), view(0, 0), self.left)

    def forward(self):
        view = self.view
        self.last = self.links.phase(self.both)
        self.r0.arrived()
        self.last.send(view(3, 0), view(3, 0), self.right)
        self.l1.arrived()
        self.last.send(view(1, 1), view(1, 1), self.left)

    def finish(self):
        self.second.arrived()
        self.last.arrived()


class RingSum:
    def __init__(self, links, part, out_buf, in_buf, right, left):
        self.links, self.part, self.out, self.inn = links, part, out_buf, in_buf
        self.right, self.left = right, left

    def push(self, phase, slot, value, device):
        self.out[slot] = value.astype(BF16)
        phase.send(self.out.at[slot], self.inn.at[slot], device)

    def start_far(self):
        links = self.links
        self.p0, self.p1 = links.phase(self.out.at[0]), links.phase(self.out.at[1])
        self.rest = links.phase(self.out.at[2:6])
        self.push(self.p0, 0, self.part(2, 0), self.right)
        self.push(self.p1, 1, self.part(2, 1), self.left)

    def start_right(self):
        self.push(self.rest, 2, self.part(1, 1), self.right)

    def start_left(self):
        self.push(self.rest, 3, self.part(3, 0), self.left)

    def middle(self):
        self.p0.arrived()
        self.push(self.rest, 4, self.inn[0].astype(F32) + self.part(1, 0), self.right)
        self.p1.arrived()
        self.push(self.rest, 5, self.inn[1].astype(F32) + self.part(3, 1), self.left)

    def finish(self):
        self.rest.arrived()
        first = self.part(0, 0) + self.inn[4].astype(F32) + self.inn[3].astype(F32)
        second = self.part(0, 1) + self.inn[2].astype(F32) + self.inn[5].astype(F32)
        return first, second


def kernel(
    nz,
    history,
    out_grad,
    lengths_hbm,
    w_in_hbm,
    w_out_hbm,
    output_hbm,
    grad_input_hbm,
    grad_w_in_hbm,
    grad_w_out_hbm,
    lengths,
    w_in,
    w_out,
    output,
    grad_input,
    grad_w_in,
    grad_w_out,
    xg,
    dg,
    xh,
    xt,
    dt,
    wg,
    hid,
    slope,
    act,
    mask,
    weights,
    sslope,
    att,
    gg,
    ga,
    gated,
    gh,
    sgrad,
    term,
    sib_out,
    sib_in,
    oterm,
    iterm,
    row_stat,
    st_own,
    st_in,
    yo_out,
    yo_in,
    yi_out,
    yi_in,
    bufs_e,
    bufs_0,
    bufs_1,
    send_sem,
    recv_sem,
    local_sem,
):
    tok, share = history.shape
    half_tok = tok // 2
    width = share * NY
    me = lax.axis_index("dp")
    y = lax.axis_index("inner")
    core = lax.rem(me, 2)
    z = lax.rem(lax.div(me, 2), nz)
    x = lax.div(me, 2 * nz)
    other = 1 - core

    xs = [x] + [lax.rem(x + k, NX) for k in range(1, NX)]
    zs = [z] + [lax.rem(z + k, nz) for k in range(1, nz)]
    ys = [y] + [lax.rem(y + k, NY) for k in range(1, NY)]
    x_devices = [((xx * nz + z) * 2 + core, y) for xx in xs]
    z_devices = [((x * nz + zz) * 2 + core, y) for zz in zs]
    y_devices = [(me, yy) for yy in ys]
    sibling = ((x * nz + z) * 2 + other, y)

    def at_x(k):
        return xs[k % NX]

    def at_z(k):
        return zs[k % nz]

    def at_y(k):
        return ys[k % NY]

    def dev_x(k):
        return x_devices[k]

    def dev_z(k):
        return z_devices[k]

    def dev_y(k):
        return y_devices[k]

    links = Links(send_sem, recv_sem)

    written = []

    def write(index, source, target):
        copy = pltpu.make_async_copy(source, target, local_sem.at[2 + index])
        copy.start()
        written.append(copy)

    barrier = pltpu.get_barrier_semaphore()
    partners = (
        [sibling]
        + [dev_y(k) for k in (1, 2, 3)]
        + [dev_x(k) for k in (1, 2, 3)]
        + [dev_z(k) for k in range(1, nz)]
    )
    for device in partners:
        pl.semaphore_signal(barrier, inc=1, device_id=device, device_id_type=pl.DeviceIdType.MESH)

    small = [
        pltpu.make_async_copy(source, target, local_sem.at[6 + i])
        for i, (source, target) in enumerate(
            ((w_in_hbm, w_in), (w_out_hbm, w_out), (lengths_hbm, lengths))
        )
    ]
    for copy in small:
        copy.start()
    own_x = pltpu.make_async_copy(history, xg.at[y], local_sem.at[0])
    own_d = pltpu.make_async_copy(out_grad, dg.at[y], local_sem.at[1])
    own_x.start()
    own_d.start()
    for copy in small:
        copy.wait()
    mine = (x, z, core, slice(None))
    wg[mine + (slice(WO, COLS),)] = w_out[...]
    for head in range(2):
        places = (GATE + head * DH, head * HEAD + VALUE, head * HEAD + QUERY, head * HEAD + KEY)
        for part, target in enumerate(places):
            source = (head * 4 + part) * DH
            wg[mine + (slice(target, target + DH),)] = w_in[:, source : source + DH]
    pl.semaphore_wait(barrier, len(partners))

    def rows_of(half):
        return pl.ds(half * half_tok, half_tok)

    gather_x = RingGather(
        links,
        lambda k, half: xg.at[at_y(k), rows_of(half)],
        dev_y(1),
        dev_y(3),
        lambda half: history.at[rows_of(half)],
        xg.at[0],
    )
    gather_d = RingGather(
        links,
        lambda k, half: dg.at[at_y(k), rows_of(half)],
        dev_y(1),
        dev_y(3),
        lambda half: out_grad.at[rows_of(half)],
        dg.at[0],
    )
    z_by_distance = sorted(range(1, nz), key=lambda k: min(k, nz - k))
    z_near = [[k for k in z_by_distance if min(k, nz - k) <= 2]]
    z_near += [[k for k in z_by_distance if min(k, nz - k) > 2]] if nz > 5 else []
    z_far = [batch[::-1] for batch in z_near[::-1]]
    z_order = z_by_distance[::-1]
    x_order = (2, 1, 3)

    class WeightGather:
        def __init__(self, first, middle, end):
            self.all = pl.ds(first, end - first)
            self.ca = pl.ds(first, middle - first)
            self.cb = pl.ds(middle, end - middle) if end > middle else None

        def to_x(self, zz):
            piece = wg.at[x, zz, core, :, self.ca]
            for k in x_order:
                self.ax.send(piece, piece, dev_x(k))

        def to_z(self, xx):
            piece = wg.at[xx, z, core, :, self.cb]
            for k in z_order:
                self.bz.send(piece, piece, dev_z(k))

        def start(self):
            own_a = wg.at[x, z, core, :, self.ca]
            self.ax = links.phase(wg.at[0 : NX - 1, :, core, :, self.ca])
            self.az = []
            for batch in z_near:
                self.az.append(links.phase(wg.at[x, 0 : len(batch), core, :, self.ca]))
                for k in batch:
                    self.az[-1].send(own_a, own_a, dev_z(k))
            if self.cb:
                own_b = wg.at[x, z, core, :, self.cb]
                self.bz = links.phase(wg.at[:, 0 : nz - 1, core, :, self.cb])
                self.bx = links.phase(wg.at[0 : NX - 1, z, core, :, self.cb])
                for k in x_order:
                    self.bx.send(own_b, own_b, dev_x(k))
            self.to_x(z)
            if self.cb:
                self.to_z(x)

        def turn_b(self):
            if self.cb:
                self.bx.arrived()
                for k in x_order:
                    self.to_z(at_x(NX - k))

        def turn_a(self, *indices):
            for index in indices:
                self.az[index].arrived()
                for k in z_near[index]:
                    self.to_x(at_z(nz - k))

        def share(self):
            if self.cb:
                self.bz.arrived()
            self.ax.arrived()
            region = wg.at[:, :, core, :, self.all]
            self.shared = links.phase(region)
            self.shared.send(region, region, sibling)

        def finish(self):
            self.shared.arrived()

    group_0 = WeightGather(0, 256, HEAD)
    group_1 = WeightGather(HEAD, HEAD + 256, 2 * HEAD)
    group_g = WeightGather(GATE, GATE + 384, COLS)
    group_0.start()
    group_1.start()
    group_g.start()
    gather_x.start()

    blocks = tok // 128
    ends = []
    total = jnp.int32(0)
    for k in range(8):
        total = total + lengths[0, k]
        ends.append(total)
    for i in range(blocks):
        row = lax.broadcasted_iota(jnp.int32, (128, 128), 0) + i * 128
        begin = jnp.zeros((128, 128), jnp.int32)
        for k in range(7):
            begin = jnp.where(row >= ends[k], ends[k], begin)
        for j in range(max(0, i - 2), i + 1):
            col = lax.broadcasted_iota(jnp.int32, (128, 128), 1) + j * 128
            allowed = (col >= begin) & (col <= row)
            mask[i * 128 : (i + 1) * 128, j * 128 : (j + 1) * 128] = jnp.where(
                allowed, 1.0 / MAXLEN, 0.0
            ).astype(F32)

    far = len(z_near) - 1
    group_0.turn_b()
    group_0.turn_a(0)
    gather_x.forward()
    gather_d.start()
    group_0.turn_a(*range(1, far + 1))
    group_1.turn_b()
    group_1.turn_a(*range(far + 1))
    group_g.turn_b()
    group_g.turn_a(*range(far + 1))
    own_x.wait()
    gather_x.finish()

    def norm_rows(block, carry):
        rows = pl.ds(pl.multiple_of(block * 128, 128), 128)
        cols = [xg[k, rows, :].astype(F32) for k in range(NY)]
        mean = sum(jnp.sum(part, 1, keepdims=True) for part in cols) / width
        square = sum(jnp.sum(part * part, 1, keepdims=True) for part in cols) / width
        inverse = lax.rsqrt(square - mean * mean + EPSILON)
        row_stat[0, rows, :] = jnp.broadcast_to(mean, (128, 128))
        row_stat[1, rows, :] = jnp.broadcast_to(inverse, (128, 128))
        for k in range(NY):
            xh[rows, k * share : (k + 1) * share] = ((cols[k] - mean) * inverse).astype(BF16)
        return carry

    lax.fori_loop(0, blocks, norm_rows, 0)
    gather_d.forward()
    for k in range(NY):
        xt[k] = xh[:, k * share : (k + 1) * share].T.reshape(nz, 2, 16, tok)
    group_0.share()

    def weight_cols(first, count):
        return wg[:, :, :, :, first : first + count].reshape(width, count)

    def hidden_cols(first, count):
        block = weight_cols(first, count)
        cols = slice(first, first + count)
        for half in range(2):
            rows = rows_of(half)
            value = nn(xh[rows, :], block)
            sigma = jax.nn.sigmoid(value)
            hid[rows, cols] = value
            act[rows, cols] = (value * sigma).astype(BF16)
            slope[rows, cols] = sigma * (1.0 + value * (1.0 - sigma))

    def cols_of(base, head):
        first = head * HEAD + base
        return slice(first, first + DH)

    def band(i):
        return slice(i * 128, (i + 1) * 128), slice(max(0, i - 2) * 128, (i + 1) * 128)

    def forward(head):
        for i in range(blocks):
            rows, cols = band(i)
            score = nt(act[rows, cols_of(QUERY, head)], act[cols, cols_of(KEY, head)]) * SCALE
            sigma = jax.nn.sigmoid(score)
            seen = mask[rows, cols]
            weight = (score * sigma * seen).astype(BF16)
            weights[head, rows, cols] = weight
            sslope[head, rows, cols] = sigma * (1.0 + score * (1.0 - sigma)) * seen
            att[rows, head * DH : (head + 1) * DH] = nn(weight, act[cols, cols_of(VALUE, head)])

    group_0.finish()
    hidden_cols(0, HEAD)
    group_1.share()
    forward(0)
    group_1.finish()
    hidden_cols(HEAD, HEAD)
    group_g.share()
    forward(1)

    def columns_sum(value):
        return jnp.sum(value.T, 0, keepdims=True)

    def head_cols(head):
        return slice(head * DH, (head + 1) * DH)

    def gate_of(head):
        return act[:, GATE + head * DH : GATE + (head + 1) * DH].astype(F32)

    def spread(row_values):
        return jnp.broadcast_to(row_values, (128, tok)).T

    class RowSums:
        def __init__(self, own, inn):
            self.own, self.inn = own, inn

        def start(self, first, second):
            self.own[0:1, :] = columns_sum(first)
            self.own[1:2, :] = columns_sum(second)
            self.phase = links.phase(self.inn.at[0 : NY - 1])
            for k in x_order:
                self.phase.send(self.own, self.inn.at[y], dev_y(k))

        def finish(self):
            self.phase.arrived()
            self.inn[y] = self.own[...]
            sums = self.inn[0] + self.inn[1] + self.inn[2] + self.inn[3]
            return sums[0:1] / width, sums[1:2] / width

    att_sums = RowSums(st_own.at[0], st_in.at[0])
    norm_sums = RowSums(st_own.at[1], st_in.at[1])
    input_sums = RowSums(st_own.at[2], st_in.at[2])
    low, high = att[:, 0:DH], att[:, DH : 2 * DH]
    att_sums.start(low + high, low * low + high * high)
    group_g.finish()
    hidden_cols(GATE, 2 * DH)
    own_d.wait()
    gather_d.finish()
    for half in range(2):
        rows = rows_of(half)
        total_gg = None
        for k in range(NY):
            block = wg[k, :, :, :, WO:COLS].reshape(share, 2 * DH)
            piece = nn(dg[k, rows, :], block)
            total_gg = piece if total_gg is None else total_gg + piece
        gg[rows, :] = total_gg
    plain, cross = 0.0, 0.0
    for head in range(2):
        g = gg[:, head_cols(head)] * gate_of(head)
        plain = plain + g
        cross = cross + g * att[:, head_cols(head)]
    norm_sums.start(plain, cross)
    for k in range(NY):
        dt[k] = dg[k].T.reshape(nz, 2, 16, tok)

    mean_row, square_row = att_sums.finish()
    inv_row = lax.rsqrt(square_row - mean_row * mean_row + EPSILON)
    att_mean, att_inv = spread(mean_row), spread(inv_row)
    for head in range(2):
        cols = head_cols(head)
        att_norm = (att[:, cols] - att_mean) * att_inv
        att[:, cols] = att_norm
        gated[:, cols] = (att_norm * gate_of(head)).astype(BF16)

    def out_block(k):
        block = wg[at_y(k), :, :, :, WO:COLS].reshape(share, 2 * DH)
        for half in range(2):
            oterm[k, rows_of(half), :] = nt(gated[rows_of(half), :], block)

    ring_o = RingSum(
        links, lambda k, half: oterm[k, rows_of(half), :], yo_out, yo_in, dev_y(1), dev_y(3)
    )
    out_block(2)
    ring_o.start_far()
    for head in range(2):
        here = slice(GATE + head * DH, GATE + (head + 1) * DH)
        gh[:, here] = (gg[:, head_cols(head)] * att[:, head_cols(head)] * slope[:, here]).astype(BF16)

    class WeightSum:
        def __init__(self, first, middle, end, bufs):
            self.a, self.b = slice(first, middle), slice(middle, end)
            self.all = slice(first, end)
            self.ax, self.az = bufs[0], bufs[1]
            self.bz, self.bx = bufs[2], bufs[3]

        def multiply(self, products, own):
            everything = (slice(None), slice(None), slice(None))
            for lhs, rhs, first in products:
                count = rhs.shape[1]
                here = everything + (slice(first, first + count),)
                rows = lhs[:, :, core if own else other].reshape(width // 2, tok)
                value = nn(rows, rhs).reshape(NX, nz, 16, count)
                if own:
                    term[here] = value
                else:
                    sib_out[here] = value.astype(BF16)
            if not own:
                view = everything + (self.all,)
                self.pair = links.phase(sib_in.at[view])
                self.pair.send(sib_out.at[view], sib_in.at[view], sibling)

        def joined(self, place):
            return term[place] + sib_in[place].astype(F32)

        def join(self):
            self.pair.arrived()
            self.px, self.pz = [], []
            for batch in z_far + [(0,)]:
                self.px.append(links.phase(self.ax.at[0, 0 : len(batch)]))
                for j in batch:
                    for k in x_order:
                        place = (at_x(k), at_z(j), slice(None), self.a)
                        self.ax[0, j, k - 1] = self.joined(place).astype(BF16)
                        self.px[-1].send(self.ax.at[0, j, k - 1], self.ax.at[1, j, k - 1], dev_x(k))
            for batch in (x_order, (0,)):
                self.pz.append(links.phase(self.bz.at[0, 0 : len(batch)]))
                for j in batch:
                    for k in z_order:
                        place = (at_x(j), at_z(k), slice(None), self.b)
                        self.bz[0, j, k - 1] = self.joined(place).astype(BF16)
                        self.pz[-1].send(self.bz.at[0, j, k - 1], self.bz.at[1, j, k - 1], dev_z(k))
            self.pza, self.pxb = links.phase(self.az.at[0]), links.phase(self.bx.at[0])

        def turn_b(self):
            for batch, phase in zip((x_order, (0,)), self.pz):
                phase.arrived()
                for j in batch:
                    value = self.joined((at_x(j), z, slice(None), self.b))
                    for k in range(nz - 1):
                        value = value + self.bz[1, j, k].astype(F32)
                    if j:
                        self.bx[0, j - 1] = value.astype(BF16)
                        self.pxb.send(self.bx.at[0, j - 1], self.bx.at[1, j - 1], dev_x(j))
                    else:
                        self.own_b = value

        def turn_a(self):
            for batch, phase in zip(z_far + [(0,)], self.px):
                phase.arrived()
                for j in batch:
                    value = self.joined((x, at_z(j), slice(None), self.a))
                    for k in range(NX - 1):
                        value = value + self.ax[1, j, k].astype(F32)
                    if j:
                        self.az[0, j - 1] = value.astype(BF16)
                        self.pza.send(self.az.at[0, j - 1], self.az.at[1, j - 1], dev_z(j))
                    else:
                        self.own_a = value

        def finish(self):
            value_a, value_b = self.own_a, self.own_b
            self.pza.arrived()
            for k in range(nz - 1):
                value_a = value_a + self.az[1, k].astype(F32)
            self.pxb.arrived()
            for k in range(NX - 1):
                value_b = value_b + self.bx[1, k].astype(F32)
            return value_a, value_b

    sum_e = WeightSum(GATE, GATE + 384, COLS, bufs_e)
    sum_0 = WeightSum(0, 256, HEAD, bufs_0)
    sum_1 = WeightSum(HEAD, HEAD + 256, 2 * HEAD, bufs_1)

    def backward_rows(head):
        mine_cols = head_cols(head)
        for i in range(blocks):
            rows, cols = band(i)
            grad_weight = nt(ga[rows, mine_cols], act[cols, cols_of(VALUE, head)])
            grad_score = (grad_weight * sslope[head, rows, cols]).astype(BF16)
            sgrad[head, rows, cols] = grad_score
            grad_q = SCALE * nn(grad_score, act[cols, cols_of(KEY, head)])
            here = cols_of(QUERY, head)
            gh[rows, here] = (grad_q * slope[rows, here]).astype(BF16)

    def backward_cols(head):
        mine_cols = head_cols(head)
        for j in range(blocks):
            cols = slice(j * 128, (j + 1) * 128)
            rows = slice(j * 128, min(j + 3, blocks) * 128)
            grad_k = SCALE * tn(sgrad[head, rows, cols], act[rows, cols_of(QUERY, head)])
            grad_v = tn(weights[head, rows, cols], ga[rows, mine_cols])
            for base, value in ((KEY, grad_k), (VALUE, grad_v)):
                here = cols_of(base, head)
                gh[cols, here] = (value * slope[cols, here]).astype(BF16)

    def in_block(k):
        block = wg[at_y(k), :, :, :, 0:WO].reshape(share, WO)
        for half in range(2):
            iterm[k, rows_of(half), :] = nt(gh[rows_of(half), :], block)

    ring_i = RingSum(
        links, lambda k, half: iterm[k, rows_of(half), :], yi_out, yi_in, dev_y(1), dev_y(3)
    )

    early = [(dt, gated[...], WO), (xt, gh[:, GATE:WO], GATE)]
    sum_e.multiply(early, False)
    out_block(1)
    ring_o.start_right()
    sum_e.multiply(early, True)
    out_block(3)
    ring_o.start_left()
    sum_e.join()
    norm_mean, cross_row = norm_sums.finish()
    cross_mean = spread((cross_row - mean_row * norm_mean) * inv_row)
    norm_mean = spread(norm_mean)
    for head in range(2):
        cols = head_cols(head)
        grad_norm = gg[:, cols] * gate_of(head)
        ga[:, cols] = ((grad_norm - norm_mean - att[:, cols] * cross_mean) * att_inv).astype(BF16)
    backward_rows(0)
    backward_cols(0)
    sum_0.multiply([(xt, gh[:, 0:HEAD], 0)], False)
    sum_0.multiply([(xt, gh[:, 0:HEAD], 0)], True)
    ring_o.middle()
    backward_rows(1)
    sum_0.join()
    backward_cols(1)
    sum_1.multiply([(xt, gh[:, HEAD : 2 * HEAD], HEAD)], False)
    in_block(2)
    ring_i.start_far()
    sum_1.multiply([(xt, gh[:, HEAD : 2 * HEAD], HEAD)], True)
    sum_1.join()
    in_block(1)
    ring_i.start_right()
    in_block(3)
    ring_i.start_left()
    in_block(0)
    sum_e.turn_b()
    sum_e.turn_a()
    sum_0.turn_b()
    sum_0.turn_a()
    ring_i.middle()
    sum_1.turn_b()
    sum_1.turn_a()

    w_sum = jnp.zeros((1, WO), F32)
    for k in range(NX):
        block = wg[k, :, :, :, 0:WO].reshape(share, WO).astype(F32)
        w_sum = w_sum + jnp.sum(block, 0, keepdims=True)
    plain, cross = 0.0, 0.0
    for k in range(WO // 128):
        cols = slice(k * 128, (k + 1) * 128)
        piece = gh[:, cols].astype(F32)
        plain = plain + piece * w_sum[:, cols]
        cross = cross + piece * hid[:, cols]
    input_sums.start(plain, cross)
    out_block(0)
    for half, value in enumerate(ring_o.finish()):
        rows = rows_of(half)
        output[rows, :] = (xg[y, rows, :].astype(F32) + value).astype(BF16)
    write(0, output, output_hbm)
    row_avg, cross_avg = (spread(row) for row in input_sums.finish())
    gate_part, out_part = sum_e.finish()
    grad_w_out[:, 0:128] = gate_part[:, 256:384]
    grad_w_out[:, 128:256] = out_part
    write(1, grad_w_out, grad_w_out_hbm)
    pieces = {GATE: gate_part[:, 0:128], GATE + DH: gate_part[:, 128:256]}
    for half, value in enumerate(ring_i.finish()):
        rows = rows_of(half)
        here = slice(half * half_tok, (half + 1) * half_tok)
        for first in range(0, share, 128):
            cols = slice(first, min(first + 128, share))
            lanes = slice(0, cols.stop - cols.start)
            mean, inverse = row_stat[0, rows, lanes], row_stat[1, rows, lanes]
            normed = (xg[y, rows, cols].astype(F32) - mean) * inverse
            centred = value[:, cols] - row_avg[here, lanes] - normed * cross_avg[here, lanes]
            grad_input[rows, cols] = dg[y, rows, cols].astype(F32) + centred * inverse
    write(2, grad_input, grad_input_hbm)
    for head, group in enumerate((sum_0, sum_1)):
        low, high = group.finish()
        pieces[head * HEAD + QUERY] = low[:, 0:128]
        pieces[head * HEAD + KEY] = low[:, 128:256]
        pieces[head * HEAD + VALUE] = high
    for head in range(2):
        places = (GATE + head * DH, head * HEAD + VALUE, head * HEAD + QUERY, head * HEAD + KEY)
        for part, place in enumerate(places):
            target = (head * 4 + part) * DH
            grad_w_in[:, target : target + DH] = pieces[place]
    write(3, grad_w_in, grad_w_in_hbm)
    links.drain()
    for copy in written:
        copy.wait()


def place_kernel(*refs):
    sources, targets, held, sems = refs[:4], refs[4:8], refs[8:12], refs[12]
    inward = [pltpu.make_async_copy(sources[i], held[i], sems.at[i]) for i in range(4)]
    outward = [pltpu.make_async_copy(held[i], targets[i], sems.at[4 + i]) for i in range(4)]
    for copy in inward:
        copy.start()
    for i in range(4):
        inward[i].wait()
        outward[i].start()
    for copy in outward:
        copy.wait()


def shards(nz, history, out_grad, lengths, w_in, w_out):
    tok, share = history.shape
    width = share * NY
    half = tok // 2
    cols = WO
    vmem = pltpu.VMEM
    def sum_bufs(wa, wb):
        return [
            vmem((2, nz, NX - 1, 16, wa), BF16),
            vmem((2, nz - 1, 16, wa), BF16),
            vmem((2, NX, nz - 1, 16, wb), BF16),
            vmem((2, NX - 1, 16, wb), BF16),
        ]

    results = pl.pallas_call(
        functools.partial(kernel, nz),
        out_shape=(
            jax.ShapeDtypeStruct((tok, share), BF16),
            jax.ShapeDtypeStruct((tok, share), F32),
            jax.ShapeDtypeStruct(w_in.shape, F32),
            jax.ShapeDtypeStruct(w_out.shape[::-1], F32),
        ),
        in_specs=[
            pl.BlockSpec(memory_space=pl.ANY),
        ]
        * 5,
        out_specs=[pl.BlockSpec(memory_space=pl.ANY)] * 4,
        scratch_shapes=[
            pltpu.SMEM(lengths.shape, lengths.dtype),
            vmem(w_in.shape, BF16),
            vmem(w_out.shape[::-1], BF16),
            vmem((tok, share), BF16),
            vmem((tok, share), F32),
            vmem(w_in.shape, F32),
            vmem(w_out.shape[::-1], F32),
            vmem((NY, tok, share), BF16),
            vmem((NY, tok, share), BF16),
            vmem((tok, width), BF16),
            vmem((NX, nz, 2, 16, tok), BF16),
            vmem((NX, nz, 2, 16, tok), BF16),
            vmem((NX, nz, 2, 16, COLS), BF16),
            vmem((tok, cols), F32),
            vmem((tok, cols), F32),
            vmem((tok, cols), BF16),
            vmem((tok, tok), F32),
            vmem((2, tok, tok), BF16),
            vmem((2, tok, tok), F32),
            vmem((tok, 2 * DH), F32),
            vmem((tok, 2 * DH), F32),
            vmem((tok, 2 * DH), BF16),
            vmem((tok, 2 * DH), BF16),
            vmem((tok, cols), BF16),
            vmem((2, tok, tok), BF16),
            vmem((NX, nz, 16, COLS), F32),
            vmem((NX, nz, 16, COLS), BF16),
            vmem((NX, nz, 16, COLS), BF16),
            vmem((NY, tok, share), F32),
            vmem((NY, tok, share), F32),
            vmem((2, tok, 128), F32),
            vmem((3, 8, tok), F32),
            vmem((3, NY, 8, tok), F32),
            vmem((6, half, share), BF16),
            vmem((6, half, share), BF16),
            vmem((6, half, share), BF16),
            vmem((6, half, share), BF16),
            sum_bufs(384, 128),
            sum_bufs(256, 128),
            sum_bufs(256, 128),
            pltpu.SemaphoreType.DMA((N_SEM,)),
            pltpu.SemaphoreType.DMA((N_SEM,)),
            pltpu.SemaphoreType.DMA((9,)),
        ],
        compiler_params=pltpu.CompilerParams(
            collective_id=0, has_side_effects=True, vmem_limit_bytes=60 * 1024 * 1024
        ),
    )(history, out_grad, lengths, w_in, w_out.T)
    anywhere = pl.BlockSpec(memory_space=pl.ANY)
    output, grad_input, grad_w_in, grad_w_out = pl.pallas_call(
        place_kernel,
        out_shape=[jax.ShapeDtypeStruct(r.shape, r.dtype) for r in results],
        in_specs=[anywhere] * 4,
        out_specs=[anywhere] * 4,
        scratch_shapes=[vmem(r.shape, r.dtype) for r in results] + [pltpu.SemaphoreType.DMA((8,))],
    )(*results)
    return output, grad_input, grad_w_in, grad_w_out.T


def solution(mesh):
    nz = mesh.shape["dp"] // (2 * NX)
    in_specs = (
        P("dp", "inner"),
        P("dp", "inner"),
        P("dp", None),
        P("dp", "inner"),
        P("inner", "dp"),
    )
    out_specs = (P("dp", "inner"), P("dp", "inner"), P("dp", "inner"), P("inner", "dp"))
    return jax.shard_map(
        functools.partial(shards, nz), mesh=mesh, in_specs=in_specs, out_specs=out_specs, check_vma=False
    )
```

```python
import functools

import jax
import jax.numpy as jnp
from jax import lax
from jax.experimental import pallas as pl
from jax.experimental.pallas import tpu as pltpu
from jax.sharding import PartitionSpec as P

H = 8
DH = 128
MAXLEN = 256
EPSILON = 1e-06
SCALE = DH ** (-0.5)
F32 = jnp.float32
BF16 = jnp.bfloat16
NX = 4
NY = 4
N_SEM = 59

HEAD = 3 * DH
QUERY, KEY, VALUE = 0, DH, 2 * DH
GATE, WO, COLS = 768, 1024, 1280


def nn(a, b):
    return lax.dot_general(a, b, (((1,), (0,)), ((), ())), preferred_element_type=F32)


def nt(a, b):
    return lax.dot_general(a, b, (((1,), (1,)), ((), ())), preferred_element_type=F32)


def tn(a, b):
    return lax.dot_general(a, b, (((0,), (0,)), ((), ())), preferred_element_type=F32)


class Links:
    def __init__(self, send_sem, recv_sem):
        self.send_sem, self.recv_sem, self.phases, self.drained = send_sem, recv_sem, [], 0

    def phase(self, region):
        return Phase(self, region)

    def drain(self):
        for phase in self.phases[self.drained :]:
            phase.sent()
        self.drained = len(self.phases)


class Phase:
    def __init__(self, links, region):
        index = len(links.phases)
        assert index < N_SEM
        links.phases.append(self)
        self.sems = dict(send_sem=links.send_sem.at[index], recv_sem=links.recv_sem.at[index])
        self.region = region

    def copy(self, source, target, device):
        return pltpu.make_async_remote_copy(
            src_ref=source,
            dst_ref=target,
            device_id=device,
            device_id_type=pl.DeviceIdType.MESH,
            **self.sems,
        )

    def send(self, source, target, device):
        self.device = device
        self.copy(source, target, device).start()

    def arrived(self):
        self.copy(self.region, self.region, self.device).wait_recv()

    def sent(self):
        self.copy(self.region, self.region, self.device).wait_send()


class RingGather:
    def __init__(self, links, view, right, left, source, both):
        self.links, self.view, self.right, self.left = links, view, right, left
        self.source, self.both = source, both

    def start(self):
        view, source, links = self.view, self.source, self.links
        self.r0, self.l1 = links.phase(view(0, 0)), links.phase(view(0, 1))
        self.second = links.phase(self.both)
        self.r0.send(source(0), view(0, 0), self.right)
        self.l1.send(source(1), view(0, 1), self.left)
        self.second.send(source(1), view(0, 1), self.right)
        self.second.send(source(0), view(0, 0), self.left)

    def forward(self):
        view = self.view
        self.last = self.links.phase(self.both)
        self.r0.arrived()
        self.last.send(view(3, 0), view(3, 0), self.right)
        self.l1.arrived()
        self.last.send(view(1, 1), view(1, 1), self.left)

    def finish(self):
        self.second.arrived()
        self.last.arrived()


class RingSum:
    def __init__(self, links, make, part, out_buf, in_buf, right, left):
        self.make = make
        self.links, self.part, self.out, self.inn = links, part, out_buf, in_buf
        self.right, self.left = right, left

    def push(self, phase, slot, value, device):
        self.out[slot] = value.astype(BF16)
        phase.send(self.out.at[slot], self.inn.at[slot], device)

    def start_far(self):
        links = self.links
        self.p0, self.p1 = links.phase(self.out.at[0]), links.phase(self.out.at[1])
        self.rest = links.phase(self.out.at[2:6])
        self.make(2, (0,))
        self.push(self.p0, 0, self.part(2, 0), self.right)
        self.make(2, (1,))
        self.push(self.p1, 1, self.part(2, 1), self.left)

    def start_right(self):
        self.make(1, (1, 0))
        self.push(self.rest, 2, self.part(1, 1), self.right)

    def start_left(self):
        self.make(3, (0, 1))
        self.push(self.rest, 3, self.part(3, 0), self.left)

    def middle(self):
        self.p0.arrived()
        self.push(self.rest, 4, self.inn[0].astype(F32) + self.part(1, 0), self.right)
        self.p1.arrived()
        self.push(self.rest, 5, self.inn[1].astype(F32) + self.part(3, 1), self.left)

    def finish(self):
        self.rest.arrived()
        first = self.part(0, 0) + self.inn[4].astype(F32) + self.inn[3].astype(F32)
        second = self.part(0, 1) + self.inn[2].astype(F32) + self.inn[5].astype(F32)
        return first, second


def kernel(
    nz,
    history,
    out_grad,
    lengths_hbm,
    w_in_hbm,
    w_out_hbm,
    output_hbm,
    grad_input_hbm,
    grad_w_in_hbm,
    grad_w_out_hbm,
    lengths,
    w_in,
    w_out,
    output,
    grad_input,
    grad_w_in,
    grad_w_out,
    xg,
    dg,
    xh,
    xt,
    dt,
    wg,
    hid,
    slope,
    act,
    mask,
    weights,
    sslope,
    att,
    gg,
    ga,
    gated,
    gh,
    sgrad,
    term,
    sib_out,
    sib_in,
    oterm,
    iterm,
    row_stat,
    st_own,
    st_in,
    yo_out,
    yo_in,
    yi_out,
    yi_in,
    bufs_e,
    bufs_0,
    bufs_1,
    send_sem,
    recv_sem,
    local_sem,
):
    tok, share = history.shape
    half_tok = tok // 2
    width = share * NY
    me = lax.axis_index("dp")
    y = lax.axis_index("inner")
    core = lax.rem(me, 2)
    z = lax.rem(lax.div(me, 2), nz)
    x = lax.div(me, 2 * nz)
    other = 1 - core

    xs = [x] + [lax.rem(x + k, NX) for k in range(1, NX)]
    zs = [z] + [lax.rem(z + k, nz) for k in range(1, nz)]
    ys = [y] + [lax.rem(y + k, NY) for k in range(1, NY)]
    x_devices = [((xx * nz + z) * 2 + core, y) for xx in xs]
    z_devices = [((x * nz + zz) * 2 + core, y) for zz in zs]
    y_devices = [(me, yy) for yy in ys]
    sibling = ((x * nz + z) * 2 + other, y)

    def at_x(k):
        return xs[k % NX]

    def at_z(k):
        return zs[k % nz]

    def at_y(k):
        return ys[k % NY]

    def dev_x(k):
        return x_devices[k]

    def dev_z(k):
        return z_devices[k]

    def dev_y(k):
        return y_devices[k]

    links = Links(send_sem, recv_sem)

    written = []

    def write(index, source, target):
        copy = pltpu.make_async_copy(source, target, local_sem.at[2 + index])
        copy.start()
        written.append(copy)

    barrier = pltpu.get_barrier_semaphore()
    partners = (
        [dev_z(k) for k in sorted(range(1, nz), key=lambda k: -min(k, nz - k))]
        + [dev_x(k) for k in (2, 1, 3)]
        + [dev_y(k) for k in (2, 1, 3)]
        + [sibling]
    )
    for device in partners:
        pl.semaphore_signal(barrier, inc=1, device_id=device, device_id_type=pl.DeviceIdType.MESH)

    small = [
        pltpu.make_async_copy(source, target, local_sem.at[6 + i])
        for i, (source, target) in enumerate(
            ((w_in_hbm, w_in), (w_out_hbm, w_out), (lengths_hbm, lengths))
        )
    ]
    for copy in small:
        copy.start()
    own_x = pltpu.make_async_copy(history, xg.at[y], local_sem.at[0])
    own_d = pltpu.make_async_copy(out_grad, dg.at[y], local_sem.at[1])
    own_x.start()
    own_d.start()
    for copy in small:
        copy.wait()
    mine = (x, z, core, slice(None))
    wg[mine + (slice(WO, COLS),)] = w_out[...]
    for head in range(2):
        places = (GATE + head * DH, head * HEAD + VALUE, head * HEAD + QUERY, head * HEAD + KEY)
        for part, target in enumerate(places):
            source = (head * 4 + part) * DH
            wg[mine + (slice(target, target + DH),)] = w_in[:, source : source + DH]
    pl.semaphore_wait(barrier, len(partners))

    def rows_of(half):
        return pl.ds(half * half_tok, half_tok)

    gather_x = RingGather(
        links,
        lambda k, half: xg.at[at_y(k), rows_of(half)],
        dev_y(1),
        dev_y(3),
        lambda half: history.at[rows_of(half)],
        xg.at[0],
    )
    gather_d = RingGather(
        links,
        lambda k, half: dg.at[at_y(k), rows_of(half)],
        dev_y(1),
        dev_y(3),
        lambda half: out_grad.at[rows_of(half)],
        dg.at[0],
    )
    z_by_distance = sorted(range(1, nz), key=lambda k: min(k, nz - k))
    z_near = [[k for k in z_by_distance if min(k, nz - k) <= 2]]
    z_near += [[k for k in z_by_distance if min(k, nz - k) > 2]] if nz > 5 else []
    z_far = [batch[::-1] for batch in z_near[::-1]]
    z_order = z_by_distance[::-1]
    x_order = (2, 1, 3)

    class WeightGather:
        def __init__(self, first, middle, end):
            self.all = pl.ds(first, end - first)
            self.ca = pl.ds(first, middle - first)
            self.cb = pl.ds(middle, end - middle) if end > middle else None

        def to_x(self, zz):
            piece = wg.at[x, zz, core, :, self.ca]
            for k in x_order:
                self.ax.send(piece, piece, dev_x(k))

        def to_z(self, xx):
            piece = wg.at[xx, z, core, :, self.cb]
            for k in z_order:
                self.bz.send(piece, piece, dev_z(k))

        def start(self):
            own_a = wg.at[x, z, core, :, self.ca]
            self.ax = links.phase(wg.at[0 : NX - 1, :, core, :, self.ca])
            self.az = []
            for batch in z_near:
                self.az.append(links.phase(wg.at[x, 0 : len(batch), core, :, self.ca]))
                for k in batch:
                    self.az[-1].send(own_a, own_a, dev_z(k))
            if self.cb:
                own_b = wg.at[x, z, core, :, self.cb]
                self.bz = links.phase(wg.at[:, 0 : nz - 1, core, :, self.cb])
                self.bx = links.phase(wg.at[0 : NX - 1, z, core, :, self.cb])
                for k in x_order:
                    self.bx.send(own_b, own_b, dev_x(k))
            self.to_x(z)
            if self.cb:
                self.to_z(x)

        def turn_b(self):
            if self.cb:
                self.bx.arrived()
                for k in x_order:
                    self.to_z(at_x(NX - k))

        def turn_a(self, *indices):
            for index in indices:
                self.az[index].arrived()
                for k in z_near[index]:
                    self.to_x(at_z(nz - k))

        def share(self):
            if self.cb:
                self.bz.arrived()
            self.ax.arrived()
            region = wg.at[:, :, core, :, self.all]
            self.shared = links.phase(region)
            self.shared.send(region, region, sibling)

        def finish(self):
            self.shared.arrived()

    group_0 = WeightGather(0, 256, HEAD)
    group_1 = WeightGather(HEAD, HEAD + 256, 2 * HEAD)
    group_g = WeightGather(GATE, GATE + 384, COLS)
    group_0.start()
    group_1.start()
    gather_x.start()

    blocks = tok // 128
    ends = []
    total = jnp.int32(0)
    for k in range(8):
        total = total + lengths[0, k]
        ends.append(total)
    for i in range(blocks):
        row = lax.broadcasted_iota(jnp.int32, (128, 128), 0) + i * 128
        begin = jnp.zeros((128, 128), jnp.int32)
        for k in range(7):
            begin = jnp.where(row >= ends[k], ends[k], begin)
        for j in range(max(0, i - 2), i + 1):
            col = lax.broadcasted_iota(jnp.int32, (128, 128), 1) + j * 128
            allowed = (col >= begin) & (col <= row)
            mask[i * 128 : (i + 1) * 128, j * 128 : (j + 1) * 128] = jnp.where(
                allowed, 1.0 / MAXLEN, 0.0
            ).astype(F32)

    far = len(z_near) - 1
    group_0.turn_b()
    group_0.turn_a(0)
    group_g.start()
    gather_x.forward()
    gather_d.start()
    group_0.turn_a(*range(1, far + 1))
    group_1.turn_b()
    group_1.turn_a(*range(far + 1))
    group_g.turn_b()
    group_g.turn_a(*range(far + 1))
    own_x.wait()
    gather_x.finish()

    def norm_rows(block, carry):
        rows = pl.ds(pl.multiple_of(block * 128, 128), 128)
        cols = [xg[k, rows, :].astype(F32) for k in range(NY)]
        mean = sum(jnp.sum(part, 1, keepdims=True) for part in cols) / width
        square = sum(jnp.sum(part * part, 1, keepdims=True) for part in cols) / width
        inverse = lax.rsqrt(square - mean * mean + EPSILON)
        row_stat[0, rows, :] = jnp.broadcast_to(mean, (128, 128))
        row_stat[1, rows, :] = jnp.broadcast_to(inverse, (128, 128))
        for k in range(NY):
            xh[rows, k * share : (k + 1) * share] = ((cols[k] - mean) * inverse).astype(BF16)
        return carry

    gather_d.forward()
    group_0.share()
    lax.fori_loop(0, blocks, norm_rows, 0)
    for k in range(NY):
        xt[k] = xh[:, k * share : (k + 1) * share].T.reshape(nz, 2, 16, tok)

    def weight_cols(first, count):
        return wg[:, :, :, :, first : first + count].reshape(width, count)

    def hidden_cols(first, count):
        block = weight_cols(first, count)
        cols = slice(first, first + count)
        for half in range(2):
            rows = rows_of(half)
            value = nn(xh[rows, :], block)
            sigma = jax.nn.sigmoid(value)
            hid[rows, cols] = value
            act[rows, cols] = (value * sigma).astype(BF16)
            slope[rows, cols] = sigma * (1.0 + value * (1.0 - sigma))

    def cols_of(base, head):
        first = head * HEAD + base
        return slice(first, first + DH)

    def band(i):
        return slice(i * 128, (i + 1) * 128), slice(max(0, i - 2) * 128, (i + 1) * 128)

    def forward(head):
        for i in range(blocks):
            rows, cols = band(i)
            score = nt(act[rows, cols_of(QUERY, head)], act[cols, cols_of(KEY, head)]) * SCALE
            sigma = jax.nn.sigmoid(score)
            seen = mask[rows, cols]
            weight = (score * sigma * seen).astype(BF16)
            weights[head, rows, cols] = weight
            sslope[head, rows, cols] = sigma * (1.0 + score * (1.0 - sigma)) * seen
            att[rows, head * DH : (head + 1) * DH] = nn(weight, act[cols, cols_of(VALUE, head)])

    group_0.finish()
    hidden_cols(0, HEAD)
    group_1.share()
    forward(0)
    group_1.finish()
    hidden_cols(HEAD, HEAD)
    group_g.share()
    forward(1)

    def columns_sum(value):
        return jnp.sum(value.T, 0, keepdims=True)

    def head_cols(head):
        return slice(head * DH, (head + 1) * DH)

    def gate_of(head):
        return act[:, GATE + head * DH : GATE + (head + 1) * DH].astype(F32)

    def spread(row_values):
        return jnp.broadcast_to(row_values, (128, tok)).T

    class RowSums:
        def __init__(self, own, inn):
            self.own, self.inn = own, inn

        def start(self, first, second):
            self.own[0:1, :] = columns_sum(first)
            self.own[1:2, :] = columns_sum(second)
            self.phase = links.phase(self.inn.at[0 : NY - 1])
            for k in x_order:
                self.phase.send(self.own, self.inn.at[y], dev_y(k))

        def finish(self):
            self.phase.arrived()
            self.inn[y] = self.own[...]
            sums = self.inn[0] + self.inn[1] + self.inn[2] + self.inn[3]
            return sums[0:1] / width, sums[1:2] / width

    att_sums = RowSums(st_own.at[0], st_in.at[0])
    norm_sums = RowSums(st_own.at[1], st_in.at[1])
    input_sums = RowSums(st_own.at[2], st_in.at[2])
    low, high = att[:, 0:DH], att[:, DH : 2 * DH]
    att_sums.start(low + high, low * low + high * high)
    group_g.finish()
    hidden_cols(GATE, 2 * DH)
    own_d.wait()
    gather_d.finish()
    for half in range(2):
        rows = rows_of(half)
        total_gg = None
        for k in range(NY):
            block = wg[k, :, :, :, WO:COLS].reshape(share, 2 * DH)
            piece = nn(dg[k, rows, :], block)
            total_gg = piece if total_gg is None else total_gg + piece
        gg[rows, :] = total_gg
    plain, cross = 0.0, 0.0
    for head in range(2):
        g = gg[:, head_cols(head)] * gate_of(head)
        plain = plain + g
        cross = cross + g * att[:, head_cols(head)]
    norm_sums.start(plain, cross)
    for k in range(NY):
        dt[k] = dg[k].T.reshape(nz, 2, 16, tok)

    mean_row, square_row = att_sums.finish()
    inv_row = lax.rsqrt(square_row - mean_row * mean_row + EPSILON)
    att_mean, att_inv = spread(mean_row), spread(inv_row)
    for head in range(2):
        cols = head_cols(head)
        att_norm = (att[:, cols] - att_mean) * att_inv
        att[:, cols] = att_norm
        gated[:, cols] = (att_norm * gate_of(head)).astype(BF16)

    def out_block(k, halves=(0, 1)):
        block = wg[at_y(k), :, :, :, WO:COLS].reshape(share, 2 * DH)
        for half in halves:
            oterm[k, rows_of(half), :] = nt(gated[rows_of(half), :], block)

    ring_o = RingSum(
        links, out_block, lambda k, half: oterm[k, rows_of(half), :], yo_out, yo_in, dev_y(1), dev_y(3)
    )
    ring_o.start_far()
    for head in range(2):
        here = slice(GATE + head * DH, GATE + (head + 1) * DH)
        gh[:, here] = (gg[:, head_cols(head)] * att[:, head_cols(head)] * slope[:, here]).astype(BF16)

    class WeightSum:
        def __init__(self, first, middle, end, bufs):
            self.a, self.b = slice(first, middle), slice(middle, end)
            self.all = slice(first, end)
            self.ax, self.az = bufs[0], bufs[1]
            self.bz, self.bx = bufs[2], bufs[3]

        def multiply(self, products, own):
            everything = (slice(None), slice(None), slice(None))
            for lhs, rhs, first in products:
                count = rhs.shape[1]
                here = everything + (slice(first, first + count),)
                rows = lhs[:, :, core if own else other].reshape(width // 2, tok)
                value = nn(rows, rhs).reshape(NX, nz, 16, count)
                if own:
                    term[here] = value
                else:
                    sib_out[here] = value.astype(BF16)
            if not own:
                view = everything + (self.all,)
                self.pair = links.phase(sib_in.at[view])
                self.pair.send(sib_out.at[view], sib_in.at[view], sibling)

        def joined(self, place):
            return term[place] + sib_in[place].astype(F32)

        def join(self):
            self.pair.arrived()
            self.px, self.pz = [], []
            for batch in z_far + [(0,)]:
                self.px.append(links.phase(self.ax.at[0, 0 : len(batch)]))
                for j in batch:
                    for k in x_order:
                        place = (at_x(k), at_z(j), slice(None), self.a)
                        self.ax[0, j, k - 1] = self.joined(place).astype(BF16)
                        self.px[-1].send(self.ax.at[0, j, k - 1], self.ax.at[1, j, k - 1], dev_x(k))
            for batch in (x_order, (0,)):
                self.pz.append(links.phase(self.bz.at[0, 0 : len(batch)]))
                for j in batch:
                    for k in z_order:
                        place = (at_x(j), at_z(k), slice(None), self.b)
                        self.bz[0, j, k - 1] = self.joined(place).astype(BF16)
                        self.pz[-1].send(self.bz.at[0, j, k - 1], self.bz.at[1, j, k - 1], dev_z(k))
            self.pza, self.pxb = links.phase(self.az.at[0]), links.phase(self.bx.at[0])

        def turn_b(self):
            for batch, phase in zip((x_order, (0,)), self.pz):
                phase.arrived()
                for j in batch:
                    value = self.joined((at_x(j), z, slice(None), self.b))
                    for k in range(nz - 1):
                        value = value + self.bz[1, j, k].astype(F32)
                    if j:
                        self.bx[0, j - 1] = value.astype(BF16)
                        self.pxb.send(self.bx.at[0, j - 1], self.bx.at[1, j - 1], dev_x(j))
                    else:
                        self.own_b = value

        def turn_a(self):
            for batch, phase in zip(z_far + [(0,)], self.px):
                phase.arrived()
                for j in batch:
                    value = self.joined((x, at_z(j), slice(None), self.a))
                    for k in range(NX - 1):
                        value = value + self.ax[1, j, k].astype(F32)
                    if j:
                        self.az[0, j - 1] = value.astype(BF16)
                        self.pza.send(self.az.at[0, j - 1], self.az.at[1, j - 1], dev_z(j))
                    else:
                        self.own_a = value

        def finish(self):
            value_a, value_b = self.own_a, self.own_b
            self.pza.arrived()
            for k in range(nz - 1):
                value_a = value_a + self.az[1, k].astype(F32)
            self.pxb.arrived()
            for k in range(NX - 1):
                value_b = value_b + self.bx[1, k].astype(F32)
            return value_a, value_b

    sum_e = WeightSum(GATE, GATE + 384, COLS, bufs_e)
    sum_0 = WeightSum(0, 256, HEAD, bufs_0)
    sum_1 = WeightSum(HEAD, HEAD + 256, 2 * HEAD, bufs_1)

    def backward_rows(head):
        mine_cols = head_cols(head)
        for i in range(blocks):
            rows, cols = band(i)
            grad_weight = nt(ga[rows, mine_cols], act[cols, cols_of(VALUE, head)])
            grad_score = (grad_weight * sslope[head, rows, cols]).astype(BF16)
            sgrad[head, rows, cols] = grad_score
            grad_q = SCALE * nn(grad_score, act[cols, cols_of(KEY, head)])
            here = cols_of(QUERY, head)
            gh[rows, here] = (grad_q * slope[rows, here]).astype(BF16)

    def backward_cols(head):
        mine_cols = head_cols(head)
        for j in range(blocks):
            cols = slice(j * 128, (j + 1) * 128)
            rows = slice(j * 128, min(j + 3, blocks) * 128)
            grad_k = SCALE * tn(sgrad[head, rows, cols], act[rows, cols_of(QUERY, head)])
            grad_v = tn(weights[head, rows, cols], ga[rows, mine_cols])
            for base, value in ((KEY, grad_k), (VALUE, grad_v)):
                here = cols_of(base, head)
                gh[cols, here] = (value * slope[cols, here]).astype(BF16)

    def in_block(k, halves=(0, 1)):
        block = wg[at_y(k), :, :, :, 0:WO].reshape(share, WO)
        for half in halves:
            iterm[k, rows_of(half), :] = nt(gh[rows_of(half), :], block)

    ring_i = RingSum(
        links, in_block, lambda k, half: iterm[k, rows_of(half), :], yi_out, yi_in, dev_y(1), dev_y(3)
    )

    early = [(dt, gated[...], WO), (xt, gh[:, GATE:WO], GATE)]
    sum_e.multiply(early, False)
    ring_o.start_right()
    sum_e.multiply(early, True)
    ring_o.start_left()
    sum_e.join()
    norm_mean, cross_row = norm_sums.finish()
    cross_mean = spread((cross_row - mean_row * norm_mean) * inv_row)
    norm_mean = spread(norm_mean)
    for head in range(2):
        cols = head_cols(head)
        grad_norm = gg[:, cols] * gate_of(head)
        ga[:, cols] = ((grad_norm - norm_mean - att[:, cols] * cross_mean) * att_inv).astype(BF16)
    backward_rows(0)
    backward_cols(0)
    sum_0.multiply([(xt, gh[:, 0:HEAD], 0)], False)
    sum_0.multiply([(xt, gh[:, 0:HEAD], 0)], True)
    ring_o.middle()
    backward_rows(1)
    sum_0.join()
    backward_cols(1)
    sum_1.multiply([(xt, gh[:, HEAD : 2 * HEAD], HEAD)], False)
    ring_i.start_far()
    sum_1.multiply([(xt, gh[:, HEAD : 2 * HEAD], HEAD)], True)
    sum_1.join()
    ring_i.start_right()
    ring_i.start_left()
    in_block(0)
    sum_e.turn_b()
    sum_e.turn_a()
    sum_0.turn_b()
    sum_0.turn_a()
    ring_i.middle()
    sum_1.turn_b()
    sum_1.turn_a()

    w_sum = jnp.zeros((1, WO), F32)
    for k in range(NX):
        block = wg[k, :, :, :, 0:WO].reshape(share, WO).astype(F32)
        w_sum = w_sum + jnp.sum(block, 0, keepdims=True)
    plain, cross = 0.0, 0.0
    for k in range(WO // 128):
        cols = slice(k * 128, (k + 1) * 128)
        piece = gh[:, cols].astype(F32)
        plain = plain + piece * w_sum[:, cols]
        cross = cross + piece * hid[:, cols]
    input_sums.start(plain, cross)
    out_block(0)
    for half, value in enumerate(ring_o.finish()):
        rows = rows_of(half)
        output[rows, :] = (xg[y, rows, :].astype(F32) + value).astype(BF16)
    write(0, output, output_hbm)
    row_avg, cross_avg = (spread(row) for row in input_sums.finish())
    gate_part, out_part = sum_e.finish()
    grad_w_out[:, 0:128] = gate_part[:, 256:384]
    grad_w_out[:, 128:256] = out_part
    write(1, grad_w_out, grad_w_out_hbm)
    pieces = {GATE: gate_part[:, 0:128], GATE + DH: gate_part[:, 128:256]}
    for half, value in enumerate(ring_i.finish()):
        rows = rows_of(half)
        here = slice(half * half_tok, (half + 1) * half_tok)
        for first in range(0, share, 128):
            cols = slice(first, min(first + 128, share))
            lanes = slice(0, cols.stop - cols.start)
            mean, inverse = row_stat[0, rows, lanes], row_stat[1, rows, lanes]
            normed = (xg[y, rows, cols].astype(F32) - mean) * inverse
            centred = value[:, cols] - row_avg[here, lanes] - normed * cross_avg[here, lanes]
            grad_input[rows, cols] = dg[y, rows, cols].astype(F32) + centred * inverse
    write(2, grad_input, grad_input_hbm)
    for head, group in enumerate((sum_0, sum_1)):
        low, high = group.finish()
        pieces[head * HEAD + QUERY] = low[:, 0:128]
        pieces[head * HEAD + KEY] = low[:, 128:256]
        pieces[head * HEAD + VALUE] = high
    for head in range(2):
        places = (GATE + head * DH, head * HEAD + VALUE, head * HEAD + QUERY, head * HEAD + KEY)
        for part, place in enumerate(places):
            target = (head * 4 + part) * DH
            grad_w_in[:, target : target + DH] = pieces[place]
    write(3, grad_w_in, grad_w_in_hbm)
    links.drain()
    for copy in written:
        copy.wait()


def place_kernel(*refs):
    sources, targets, held, sems = refs[:4], refs[4:8], refs[8:12], refs[12]
    inward = [pltpu.make_async_copy(sources[i], held[i], sems.at[i]) for i in range(4)]
    outward = [pltpu.make_async_copy(held[i], targets[i], sems.at[4 + i]) for i in range(4)]
    for copy in inward:
        copy.start()
    for i in range(4):
        inward[i].wait()
        outward[i].start()
    for copy in outward:
        copy.wait()


def shards(nz, history, out_grad, lengths, w_in, w_out):
    tok, share = history.shape
    width = share * NY
    half = tok // 2
    cols = WO
    vmem = pltpu.VMEM
    def sum_bufs(wa, wb):
        return [
            vmem((2, nz, NX - 1, 16, wa), BF16),
            vmem((2, nz - 1, 16, wa), BF16),
            vmem((2, NX, nz - 1, 16, wb), BF16),
            vmem((2, NX - 1, 16, wb), BF16),
        ]

    results = pl.pallas_call(
        functools.partial(kernel, nz),
        out_shape=(
            jax.ShapeDtypeStruct((tok, share), BF16),
            jax.ShapeDtypeStruct((tok, share), F32),
            jax.ShapeDtypeStruct(w_in.shape, F32),
            jax.ShapeDtypeStruct(w_out.shape[::-1], F32),
        ),
        in_specs=[
            pl.BlockSpec(memory_space=pl.ANY),
        ]
        * 5,
        out_specs=[pl.BlockSpec(memory_space=pl.ANY)] * 4,
        scratch_shapes=[
            pltpu.SMEM(lengths.shape, lengths.dtype),
            vmem(w_in.shape, BF16),
            vmem(w_out.shape[::-1], BF16),
            vmem((tok, share), BF16),
            vmem((tok, share), F32),
            vmem(w_in.shape, F32),
            vmem(w_out.shape[::-1], F32),
            vmem((NY, tok, share), BF16),
            vmem((NY, tok, share), BF16),
            vmem((tok, width), BF16),
            vmem((NX, nz, 2, 16, tok), BF16),
            vmem((NX, nz, 2, 16, tok), BF16),
            vmem((NX, nz, 2, 16, COLS), BF16),
            vmem((tok, cols), F32),
            vmem((tok, cols), F32),
            vmem((tok, cols), BF16),
            vmem((tok, tok), F32),
            vmem((2, tok, tok), BF16),
            vmem((2, tok, tok), F32),
            vmem((tok, 2 * DH), F32),
            vmem((tok, 2 * DH), F32),
            vmem((tok, 2 * DH), BF16),
            vmem((tok, 2 * DH), BF16),
            vmem((tok, cols), BF16),
            vmem((2, tok, tok), BF16),
            vmem((NX, nz, 16, COLS), F32),
            vmem((NX, nz, 16, COLS), BF16),
            vmem((NX, nz, 16, COLS), BF16),
            vmem((NY, tok, share), F32),
            vmem((NY, tok, share), F32),
            vmem((2, tok, 128), F32),
            vmem((3, 8, tok), F32),
            vmem((3, NY, 8, tok), F32),
            vmem((6, half, share), BF16),
            vmem((6, half, share), BF16),
            vmem((6, half, share), BF16),
            vmem((6, half, share), BF16),
            sum_bufs(384, 128),
            sum_bufs(256, 128),
            sum_bufs(256, 128),
            pltpu.SemaphoreType.DMA((N_SEM,)),
            pltpu.SemaphoreType.DMA((N_SEM,)),
            pltpu.SemaphoreType.DMA((9,)),
        ],
        compiler_params=pltpu.CompilerParams(
            collective_id=0, has_side_effects=True, vmem_limit_bytes=60 * 1024 * 1024
        ),
    )(history, out_grad, lengths, w_in, w_out.T)
    anywhere = pl.BlockSpec(memory_space=pl.ANY)
    output, grad_input, grad_w_in, grad_w_out = pl.pallas_call(
        place_kernel,
        out_shape=[jax.ShapeDtypeStruct(r.shape, r.dtype) for r in results],
        in_specs=[anywhere] * 4,
        out_specs=[anywhere] * 4,
        scratch_shapes=[vmem(r.shape, r.dtype) for r in results] + [pltpu.SemaphoreType.DMA((8,))],
    )(*results)
    return output, grad_input, grad_w_in, grad_w_out.T


def solution(mesh):
    nz = mesh.shape["dp"] // (2 * NX)
    in_specs = (
        P("dp", "inner"),
        P("dp", "inner"),
        P("dp", None),
        P("dp", "inner"),
        P("inner", "dp"),
    )
    out_specs = (P("dp", "inner"), P("dp", "inner"), P("dp", "inner"), P("inner", "dp"))
    return jax.shard_map(
        functools.partial(shards, nz), mesh=mesh, in_specs=in_specs, out_specs=out_specs, check_vma=False
    )
```

```python
import functools

import jax
import jax.numpy as jnp
from jax import lax
from jax.experimental import pallas as pl
from jax.experimental.pallas import tpu as pltpu
from jax.sharding import PartitionSpec as P

H = 8
DH = 128
MAXLEN = 256
EPSILON = 1e-06
SCALE = DH ** (-0.5)
F32 = jnp.float32
BF16 = jnp.bfloat16
NX = 4
NY = 4
N_SEM = 57

HEAD = 3 * DH
QUERY, KEY, VALUE = 0, DH, 2 * DH
GATE, WO, COLS = 768, 1024, 1280


def nn(a, b):
    return lax.dot_general(a, b, (((1,), (0,)), ((), ())), preferred_element_type=F32)


def nt(a, b):
    return lax.dot_general(a, b, (((1,), (1,)), ((), ())), preferred_element_type=F32)


def tn(a, b):
    return lax.dot_general(a, b, (((0,), (0,)), ((), ())), preferred_element_type=F32)


class Links:
    def __init__(self, send_sem, recv_sem):
        self.send_sem, self.recv_sem, self.phases, self.drained = send_sem, recv_sem, [], 0

    def phase(self, region):
        return Phase(self, region)

    def drain(self, count=None):
        count = len(self.phases) if count is None else count
        for phase in self.phases[self.drained : count]:
            phase.sent()
        self.drained = count


class Phase:
    def __init__(self, links, region):
        index = len(links.phases)
        assert index < N_SEM
        links.phases.append(self)
        self.sems = dict(send_sem=links.send_sem.at[index], recv_sem=links.recv_sem.at[index])
        self.region = region

    def copy(self, source, target, device):
        return pltpu.make_async_remote_copy(
            src_ref=source,
            dst_ref=target,
            device_id=device,
            device_id_type=pl.DeviceIdType.MESH,
            **self.sems,
        )

    def send(self, source, target, device):
        self.device = device
        self.copy(source, target, device).start()

    def arrived(self):
        self.copy(self.region, self.region, self.device).wait_recv()

    def sent(self):
        self.copy(self.region, self.region, self.device).wait_send()


class RingGather:
    def __init__(self, links, view, right, left, source, both):
        self.links, self.view, self.right, self.left = links, view, right, left
        self.source, self.both = source, both

    def start(self):
        view, source, links = self.view, self.source, self.links
        self.r0, self.l1 = links.phase(view(0, 0)), links.phase(view(0, 1))
        self.second = links.phase(self.both)
        self.r0.send(source(0), view(0, 0), self.right)
        self.l1.send(source(1), view(0, 1), self.left)
        self.second.send(source(1), view(0, 1), self.right)
        self.second.send(source(0), view(0, 0), self.left)

    def forward(self):
        view = self.view
        self.last = self.links.phase(self.both)
        self.r0.arrived()
        self.last.send(view(3, 0), view(3, 0), self.right)
        self.l1.arrived()
        self.last.send(view(1, 1), view(1, 1), self.left)

    def finish(self):
        self.second.arrived()
        self.last.arrived()


class RingSum:
    def __init__(self, links, make, part, out_buf, in_buf, right, left):
        self.make = make
        self.links, self.part, self.out, self.inn = links, part, out_buf, in_buf
        self.right, self.left = right, left

    def push(self, phase, slot, value, device):
        self.out[slot] = value.astype(BF16)
        phase.send(self.out.at[slot], self.inn.at[slot], device)

    def start_far(self):
        links = self.links
        self.p0, self.p1 = links.phase(self.out.at[0]), links.phase(self.out.at[1])
        self.rest = links.phase(self.out.at[2:6])
        self.make(2, (0,))
        self.push(self.p0, 0, self.part(2, 0), self.right)
        self.make(2, (1,))
        self.push(self.p1, 1, self.part(2, 1), self.left)

    def start_right(self):
        self.make(1, (1, 0))
        self.push(self.rest, 2, self.part(1, 1), self.right)

    def start_left(self):
        self.make(3, (0, 1))
        self.push(self.rest, 3, self.part(3, 0), self.left)

    def middle(self):
        self.p0.arrived()
        self.push(self.rest, 4, self.inn[0].astype(F32) + self.part(1, 0), self.right)
        self.p1.arrived()
        self.push(self.rest, 5, self.inn[1].astype(F32) + self.part(3, 1), self.left)

    def finish(self):
        self.rest.arrived()
        first = self.part(0, 0) + self.inn[4].astype(F32) + self.inn[3].astype(F32)
        second = self.part(0, 1) + self.inn[2].astype(F32) + self.inn[5].astype(F32)
        return first, second


def kernel(
    nz,
    history,
    out_grad,
    lengths_hbm,
    w_in_hbm,
    w_out_hbm,
    output_hbm,
    grad_input_hbm,
    grad_w_in_hbm,
    grad_w_out_hbm,
    lengths,
    w_in,
    w_out,
    output,
    grad_input,
    grad_w_in,
    grad_w_out,
    xg,
    dg,
    xh,
    xt,
    dt,
    wg,
    hid,
    slope,
    act,
    mask,
    weights,
    sslope,
    att,
    gg,
    ga,
    gated,
    gh,
    sgrad,
    term,
    sib_out,
    sib_in,
    oterm,
    iterm,
    row_stat,
    st_own,
    st_in,
    yo_out,
    yo_in,
    yi_out,
    yi_in,
    bufs_e,
    bufs_0,
    bufs_1,
    send_sem,
    recv_sem,
    local_sem,
):
    tok, share = history.shape
    half_tok = tok // 2
    width = share * NY
    me = lax.axis_index("dp")
    y = lax.axis_index("inner")
    core = lax.rem(me, 2)
    z = lax.rem(lax.div(me, 2), nz)
    x = lax.div(me, 2 * nz)
    other = 1 - core

    xs = [x] + [lax.rem(x + k, NX) for k in range(1, NX)]
    zs = [z] + [lax.rem(z + k, nz) for k in range(1, nz)]
    ys = [y] + [lax.rem(y + k, NY) for k in range(1, NY)]
    x_devices = [((xx * nz + z) * 2 + core, y) for xx in xs]
    z_devices = [((x * nz + zz) * 2 + core, y) for zz in zs]
    y_devices = [(me, yy) for yy in ys]
    sibling = ((x * nz + z) * 2 + other, y)

    def at_x(k):
        return xs[k % NX]

    def at_z(k):
        return zs[k % nz]

    def at_y(k):
        return ys[k % NY]

    def dev_x(k):
        return x_devices[k]

    def dev_z(k):
        return z_devices[k]

    def dev_y(k):
        return y_devices[k]

    links = Links(send_sem, recv_sem)

    written = []

    def write(index, source, target):
        copy = pltpu.make_async_copy(source, target, local_sem.at[2 + index])
        copy.start()
        written.append(copy)

    barrier = pltpu.get_barrier_semaphore()
    partners = (
        [dev_z(k) for k in sorted(range(1, nz), key=lambda k: -min(k, nz - k))]
        + [dev_x(k) for k in (2, 1, 3)]
        + [dev_y(k) for k in (2, 1, 3)]
        + [sibling]
    )
    for device in partners:
        pl.semaphore_signal(barrier, inc=1, device_id=device, device_id_type=pl.DeviceIdType.MESH)

    small = [
        pltpu.make_async_copy(source, target, local_sem.at[6 + i])
        for i, (source, target) in enumerate(
            ((w_in_hbm, w_in), (w_out_hbm, w_out), (lengths_hbm, lengths))
        )
    ]
    for copy in small:
        copy.start()
    own_x = pltpu.make_async_copy(history, xg.at[y], local_sem.at[0])
    own_d = pltpu.make_async_copy(out_grad, dg.at[y], local_sem.at[1])
    own_x.start()
    own_d.start()
    for copy in small:
        copy.wait()
    mine = (x, z, core, slice(None))
    wg[mine + (slice(WO, COLS),)] = w_out[...]
    for head in range(2):
        places = (GATE + head * DH, head * HEAD + VALUE, head * HEAD + QUERY, head * HEAD + KEY)
        for part, target in enumerate(places):
            source = (head * 4 + part) * DH
            wg[mine + (slice(target, target + DH),)] = w_in[:, source : source + DH]
    pl.semaphore_wait(barrier, len(partners))

    def rows_of(half):
        return pl.ds(half * half_tok, half_tok)

    gather_x = RingGather(
        links,
        lambda k, half: xg.at[at_y(k), rows_of(half)],
        dev_y(1),
        dev_y(3),
        lambda half: history.at[rows_of(half)],
        xg.at[0],
    )
    gather_d = RingGather(
        links,
        lambda k, half: dg.at[at_y(k), rows_of(half)],
        dev_y(1),
        dev_y(3),
        lambda half: out_grad.at[rows_of(half)],
        dg.at[0],
    )
    z_by_distance = sorted(range(1, nz), key=lambda k: min(k, nz - k))
    z_near = [[k for k in z_by_distance if min(k, nz - k) <= 2]]
    z_near += [[k for k in z_by_distance if min(k, nz - k) > 2]] if nz > 5 else []
    z_far = [batch[::-1] for batch in z_near[::-1]]
    z_order = z_by_distance[::-1]
    x_order = (2, 1, 3)

    class WeightGather:
        def __init__(self, first, middle, end):
            self.all = pl.ds(first, end - first)
            self.ca = pl.ds(first, middle - first)
            self.cb = pl.ds(middle, end - middle) if end > middle else None

        def to_x(self, zz):
            piece = wg.at[x, zz, core, :, self.ca]
            for k in x_order:
                self.ax.send(piece, piece, dev_x(k))

        def to_z(self, xx):
            piece = wg.at[xx, z, core, :, self.cb]
            for k in z_order:
                self.bz.send(piece, piece, dev_z(k))

        def start(self):
            own_a = wg.at[x, z, core, :, self.ca]
            self.ax = links.phase(wg.at[0 : NX - 1, :, core, :, self.ca])
            self.az = []
            for batch in z_near:
                self.az.append(links.phase(wg.at[x, 0 : len(batch), core, :, self.ca]))
                for k in batch:
                    self.az[-1].send(own_a, own_a, dev_z(k))
            if self.cb:
                own_b = wg.at[x, z, core, :, self.cb]
                self.bz = links.phase(wg.at[:, 0 : nz - 1, core, :, self.cb])
                self.bx = links.phase(wg.at[0 : NX - 1, z, core, :, self.cb])
                for k in x_order:
                    self.bx.send(own_b, own_b, dev_x(k))
            self.to_x(z)
            if self.cb:
                self.to_z(x)

        def turn_b(self):
            if self.cb:
                self.bx.arrived()
                for k in x_order:
                    self.to_z(at_x(NX - k))

        def turn_a(self, *indices):
            for index in indices:
                self.az[index].arrived()
                for k in z_near[index]:
                    self.to_x(at_z(nz - k))

        def share(self):
            if self.cb:
                self.bz.arrived()
            self.ax.arrived()
            region = wg.at[:, :, core, :, self.all]
            self.shared = links.phase(region)
            self.shared.send(region, region, sibling)

        def finish(self):
            self.shared.arrived()

    group_0 = WeightGather(0, 256, HEAD)
    group_1 = WeightGather(HEAD, HEAD + 256, 2 * HEAD)
    group_g = WeightGather(GATE, COLS, COLS)
    group_0.start()
    group_1.start()
    gather_x.start()

    blocks = tok // 128
    ends = []
    total = jnp.int32(0)
    for k in range(8):
        total = total + lengths[0, k]
        ends.append(total)
    for i in range(blocks):
        row = lax.broadcasted_iota(jnp.int32, (128, 128), 0) + i * 128
        begin = jnp.zeros((128, 128), jnp.int32)
        for k in range(7):
            begin = jnp.where(row >= ends[k], ends[k], begin)
        for j in range(max(0, i - 2), i + 1):
            col = lax.broadcasted_iota(jnp.int32, (128, 128), 1) + j * 128
            allowed = (col >= begin) & (col <= row)
            mask[i * 128 : (i + 1) * 128, j * 128 : (j + 1) * 128] = jnp.where(
                allowed, 1.0 / MAXLEN, 0.0
            ).astype(F32)

    far = len(z_near) - 1
    group_0.turn_b()
    group_0.turn_a(0)
    group_g.start()
    gather_x.forward()
    gather_d.start()
    group_0.turn_a(*range(1, far + 1))
    group_1.turn_b()
    group_1.turn_a(*range(far + 1))
    group_g.turn_b()
    group_g.turn_a(*range(far + 1))
    own_x.wait()
    gather_x.finish()

    def norm_rows(block, carry):
        rows = pl.ds(pl.multiple_of(block * 128, 128), 128)
        cols = [xg[k, rows, :].astype(F32) for k in range(NY)]
        mean = sum(jnp.sum(part, 1, keepdims=True) for part in cols) / width
        square = sum(jnp.sum(part * part, 1, keepdims=True) for part in cols) / width
        inverse = lax.rsqrt(square - mean * mean + EPSILON)
        row_stat[0, rows, :] = jnp.broadcast_to(mean, (128, 128))
        row_stat[1, rows, :] = jnp.broadcast_to(inverse, (128, 128))
        for k in range(NY):
            xh[rows, k * share : (k + 1) * share] = ((cols[k] - mean) * inverse).astype(BF16)
        return carry

    gather_d.forward()
    group_0.share()
    lax.fori_loop(0, blocks, norm_rows, 0)
    for k in range(NY):
        xt[k] = xh[:, k * share : (k + 1) * share].T.reshape(nz, 2, 16, tok)

    def weight_cols(first, count):
        return wg[:, :, :, :, first : first + count].reshape(width, count)

    def hidden_cols(first, count):
        block = weight_cols(first, count)
        cols = slice(first, first + count)
        for half in range(2):
            rows = rows_of(half)
            value = nn(xh[rows, :], block)
            sigma = jax.nn.sigmoid(value)
            hid[rows, cols] = value
            act[rows, cols] = (value * sigma).astype(BF16)
            slope[rows, cols] = sigma * (1.0 + value * (1.0 - sigma))

    def cols_of(base, head):
        first = head * HEAD + base
        return slice(first, first + DH)

    def band(i):
        return slice(i * 128, (i + 1) * 128), slice(max(0, i - 2) * 128, (i + 1) * 128)

    def forward(head):
        for i in range(blocks):
            rows, cols = band(i)
            score = nt(act[rows, cols_of(QUERY, head)], act[cols, cols_of(KEY, head)]) * SCALE
            sigma = jax.nn.sigmoid(score)
            seen = mask[rows, cols]
            weight = (score * sigma * seen).astype(BF16)
            weights[head, rows, cols] = weight
            sslope[head, rows, cols] = sigma * (1.0 + score * (1.0 - sigma)) * seen
            att[rows, head * DH : (head + 1) * DH] = nn(weight, act[cols, cols_of(VALUE, head)])

    group_0.finish()
    hidden_cols(0, HEAD)
    group_1.share()
    forward(0)
    group_1.finish()
    hidden_cols(HEAD, HEAD)
    group_g.share()
    forward(1)

    def columns_sum(value):
        return jnp.sum(value.T, 0, keepdims=True)

    def head_cols(head):
        return slice(head * DH, (head + 1) * DH)

    def gate_of(head):
        return act[:, GATE + head * DH : GATE + (head + 1) * DH].astype(F32)

    def spread(row_values):
        return jnp.broadcast_to(row_values, (128, tok)).T

    class RowSums:
        def __init__(self, own, inn):
            self.own, self.inn = own, inn

        def start(self, first, second):
            self.own[0:1, :] = columns_sum(first)
            self.own[1:2, :] = columns_sum(second)
            self.phase = links.phase(self.inn.at[0 : NY - 1])
            for k in x_order:
                self.phase.send(self.own, self.inn.at[y], dev_y(k))

        def finish(self):
            self.phase.arrived()
            self.inn[y] = self.own[...]
            sums = self.inn[0] + self.inn[1] + self.inn[2] + self.inn[3]
            return sums[0:1] / width, sums[1:2] / width

    att_sums = RowSums(st_own.at[0], st_in.at[0])
    norm_sums = RowSums(st_own.at[1], st_in.at[1])
    input_sums = RowSums(st_own.at[2], st_in.at[2])
    low, high = att[:, 0:DH], att[:, DH : 2 * DH]
    gathered = len(links.phases)
    att_sums.start(low + high, low * low + high * high)
    group_g.finish()
    hidden_cols(GATE, 2 * DH)
    own_d.wait()
    gather_d.finish()
    for half in range(2):
        rows = rows_of(half)
        total_gg = None
        for k in range(NY):
            block = wg[k, :, :, :, WO:COLS].reshape(share, 2 * DH)
            piece = nn(dg[k, rows, :], block)
            total_gg = piece if total_gg is None else total_gg + piece
        gg[rows, :] = total_gg
    plain, cross = 0.0, 0.0
    for head in range(2):
        g = gg[:, head_cols(head)] * gate_of(head)
        plain = plain + g
        cross = cross + g * att[:, head_cols(head)]
    norm_sums.start(plain, cross)
    for k in range(NY):
        dt[k] = dg[k].T.reshape(nz, 2, 16, tok)

    mean_row, square_row = att_sums.finish()
    inv_row = lax.rsqrt(square_row - mean_row * mean_row + EPSILON)
    att_mean, att_inv = spread(mean_row), spread(inv_row)
    for head in range(2):
        cols = head_cols(head)
        att_norm = (att[:, cols] - att_mean) * att_inv
        att[:, cols] = att_norm
        gated[:, cols] = (att_norm * gate_of(head)).astype(BF16)

    def out_block(k, halves=(0, 1)):
        block = wg[at_y(k), :, :, :, WO:COLS].reshape(share, 2 * DH)
        for half in halves:
            oterm[k, rows_of(half), :] = nt(gated[rows_of(half), :], block)

    ring_o = RingSum(
        links, out_block, lambda k, half: oterm[k, rows_of(half), :], yo_out, yo_in, dev_y(1), dev_y(3)
    )
    ring_o.start_far()
    for head in range(2):
        here = slice(GATE + head * DH, GATE + (head + 1) * DH)
        gh[:, here] = (gg[:, head_cols(head)] * att[:, head_cols(head)] * slope[:, here]).astype(BF16)

    class WeightSum:
        def __init__(self, first, middle, end, bufs):
            self.a, self.b = slice(first, middle), slice(middle, end)
            self.all = slice(first, end)
            self.ax, self.az = bufs[0], bufs[1]
            self.bz, self.bx = bufs[2], bufs[3]

        def multiply(self, products, own):
            everything = (slice(None), slice(None), slice(None))
            for lhs, rhs, first in products:
                count = rhs.shape[1]
                here = everything + (slice(first, first + count),)
                rows = lhs[:, :, core if own else other].reshape(width // 2, tok)
                value = nn(rows, rhs).reshape(NX, nz, 16, count)
                if own:
                    term[here] = value
                else:
                    sib_out[here] = value.astype(BF16)
            if not own:
                view = everything + (self.all,)
                self.pair = links.phase(sib_in.at[view])
                self.pair.send(sib_out.at[view], sib_in.at[view], sibling)

        def joined(self, place):
            return term[place] + sib_in[place].astype(F32)

        def join(self):
            self.pair.arrived()
            self.px, self.pz = [], []
            for batch in z_far + [(0,)]:
                self.px.append(links.phase(self.ax.at[0, 0 : len(batch)]))
                for j in batch:
                    for k in x_order:
                        place = (at_x(k), at_z(j), slice(None), self.a)
                        self.ax[0, j, k - 1] = self.joined(place).astype(BF16)
                        self.px[-1].send(self.ax.at[0, j, k - 1], self.ax.at[1, j, k - 1], dev_x(k))
            for batch in (x_order, (0,)):
                self.pz.append(links.phase(self.bz.at[0, 0 : len(batch)]))
                for j in batch:
                    for k in z_order:
                        place = (at_x(j), at_z(k), slice(None), self.b)
                        self.bz[0, j, k - 1] = self.joined(place).astype(BF16)
                        self.pz[-1].send(self.bz.at[0, j, k - 1], self.bz.at[1, j, k - 1], dev_z(k))
            self.pza, self.pxb = links.phase(self.az.at[0]), links.phase(self.bx.at[0])

        def turn_b(self):
            for batch, phase in zip((x_order, (0,)), self.pz):
                phase.arrived()
                for j in batch:
                    value = self.joined((at_x(j), z, slice(None), self.b))
                    for k in range(nz - 1):
                        value = value + self.bz[1, j, k].astype(F32)
                    if j:
                        self.bx[0, j - 1] = value.astype(BF16)
                        self.pxb.send(self.bx.at[0, j - 1], self.bx.at[1, j - 1], dev_x(j))
                    else:
                        self.own_b = value

        def turn_a(self):
            for batch, phase in zip(z_far + [(0,)], self.px):
                phase.arrived()
                for j in batch:
                    value = self.joined((x, at_z(j), slice(None), self.a))
                    for k in range(NX - 1):
                        value = value + self.ax[1, j, k].astype(F32)
                    if j:
                        self.az[0, j - 1] = value.astype(BF16)
                        self.pza.send(self.az.at[0, j - 1], self.az.at[1, j - 1], dev_z(j))
                    else:
                        self.own_a = value

        def finish(self):
            value_a, value_b = self.own_a, self.own_b
            self.pza.arrived()
            for k in range(nz - 1):
                value_a = value_a + self.az[1, k].astype(F32)
            self.pxb.arrived()
            for k in range(NX - 1):
                value_b = value_b + self.bx[1, k].astype(F32)
            return value_a, value_b

    sum_e = WeightSum(GATE, GATE + 384, COLS, bufs_e)
    sum_0 = WeightSum(0, 256, HEAD, bufs_0)
    sum_1 = WeightSum(HEAD, HEAD + 256, 2 * HEAD, bufs_1)

    def backward_rows(head):
        mine_cols = head_cols(head)
        for i in range(blocks):
            rows, cols = band(i)
            grad_weight = nt(ga[rows, mine_cols], act[cols, cols_of(VALUE, head)])
            grad_score = (grad_weight * sslope[head, rows, cols]).astype(BF16)
            sgrad[head, rows, cols] = grad_score
            grad_q = SCALE * nn(grad_score, act[cols, cols_of(KEY, head)])
            here = cols_of(QUERY, head)
            gh[rows, here] = (grad_q * slope[rows, here]).astype(BF16)

    def backward_cols(head):
        mine_cols = head_cols(head)
        for j in range(blocks):
            cols = slice(j * 128, (j + 1) * 128)
            rows = slice(j * 128, min(j + 3, blocks) * 128)
            grad_k = SCALE * tn(sgrad[head, rows, cols], act[rows, cols_of(QUERY, head)])
            grad_v = tn(weights[head, rows, cols], ga[rows, mine_cols])
            for base, value in ((KEY, grad_k), (VALUE, grad_v)):
                here = cols_of(base, head)
                gh[cols, here] = (value * slope[cols, here]).astype(BF16)

    def in_block(k, halves=(0, 1)):
        block = wg[at_y(k), :, :, :, 0:WO].reshape(share, WO)
        for half in halves:
            iterm[k, rows_of(half), :] = nt(gh[rows_of(half), :], block)

    ring_i = RingSum(
        links, in_block, lambda k, half: iterm[k, rows_of(half), :], yi_out, yi_in, dev_y(1), dev_y(3)
    )

    early = [(dt, gated[...], WO), (xt, gh[:, GATE:WO], GATE)]
    sum_e.multiply(early, False)
    ring_o.start_right()
    sum_e.multiply(early, True)
    ring_o.start_left()
    sum_e.join()
    links.drain(gathered)
    norm_mean, cross_row = norm_sums.finish()
    cross_mean = spread((cross_row - mean_row * norm_mean) * inv_row)
    norm_mean = spread(norm_mean)
    for head in range(2):
        cols = head_cols(head)
        grad_norm = gg[:, cols] * gate_of(head)
        ga[:, cols] = ((grad_norm - norm_mean - att[:, cols] * cross_mean) * att_inv).astype(BF16)
    backward_rows(0)
    backward_cols(0)
    sum_0.multiply([(xt, gh[:, 0:HEAD], 0)], False)
    sum_0.multiply([(xt, gh[:, 0:HEAD], 0)], True)
    ring_o.middle()
    backward_rows(1)
    sum_0.join()
    backward_cols(1)
    sum_1.multiply([(xt, gh[:, HEAD : 2 * HEAD], HEAD)], False)
    ring_i.start_far()
    sum_1.multiply([(xt, gh[:, HEAD : 2 * HEAD], HEAD)], True)
    sum_1.join()
    ring_i.start_right()
    ring_i.start_left()
    in_block(0)
    sum_e.turn_b()
    sum_e.turn_a()
    sum_0.turn_b()
    sum_0.turn_a()
    ring_i.middle()
    sum_1.turn_b()
    sum_1.turn_a()

    w_sum = jnp.zeros((1, WO), F32)
    for k in range(NX):
        block = wg[k, :, :, :, 0:WO].reshape(share, WO).astype(F32)
        w_sum = w_sum + jnp.sum(block, 0, keepdims=True)
    plain, cross = 0.0, 0.0
    for k in range(WO // 128):
        cols = slice(k * 128, (k + 1) * 128)
        piece = gh[:, cols].astype(F32)
        plain = plain + piece * w_sum[:, cols]
        cross = cross + piece * hid[:, cols]
    input_sums.start(plain, cross)
    out_block(0)
    for half, value in enumerate(ring_o.finish()):
        rows = rows_of(half)
        output[rows, :] = (xg[y, rows, :].astype(F32) + value).astype(BF16)
    write(0, output, output_hbm)
    row_avg, cross_avg = (spread(row) for row in input_sums.finish())
    gate_part, out_part = sum_e.finish()
    grad_w_out[:, 0:128] = gate_part[:, 256:384]
    grad_w_out[:, 128:256] = out_part
    write(1, grad_w_out, grad_w_out_hbm)
    pieces = {GATE: gate_part[:, 0:128], GATE + DH: gate_part[:, 128:256]}
    for half, value in enumerate(ring_i.finish()):
        rows = rows_of(half)
        here = slice(half * half_tok, (half + 1) * half_tok)
        for first in range(0, share, 128):
            cols = slice(first, min(first + 128, share))
            lanes = slice(0, cols.stop - cols.start)
            mean, inverse = row_stat[0, rows, lanes], row_stat[1, rows, lanes]
            normed = (xg[y, rows, cols].astype(F32) - mean) * inverse
            centred = value[:, cols] - row_avg[here, lanes] - normed * cross_avg[here, lanes]
            grad_input[rows, cols] = dg[y, rows, cols].astype(F32) + centred * inverse
    write(2, grad_input, grad_input_hbm)
    links.drain()
    for head, group in enumerate((sum_0, sum_1)):
        low, high = group.finish()
        pieces[head * HEAD + QUERY] = low[:, 0:128]
        pieces[head * HEAD + KEY] = low[:, 128:256]
        pieces[head * HEAD + VALUE] = high
    for head in range(2):
        places = (GATE + head * DH, head * HEAD + VALUE, head * HEAD + QUERY, head * HEAD + KEY)
        for part, place in enumerate(places):
            target = (head * 4 + part) * DH
            grad_w_in[:, target : target + DH] = pieces[place]
    write(3, grad_w_in, grad_w_in_hbm)
    links.drain()
    for copy in written:
        copy.wait()


def place_kernel(*refs):
    sources, targets, held, sems = refs[:4], refs[4:8], refs[8:12], refs[12]
    inward = [pltpu.make_async_copy(sources[i], held[i], sems.at[i]) for i in range(4)]
    outward = [pltpu.make_async_copy(held[i], targets[i], sems.at[4 + i]) for i in range(4)]
    for copy in inward:
        copy.start()
    for i in range(4):
        inward[i].wait()
        outward[i].start()
    for copy in outward:
        copy.wait()


def shards(nz, history, out_grad, lengths, w_in, w_out):
    tok, share = history.shape
    width = share * NY
    half = tok // 2
    cols = WO
    vmem = pltpu.VMEM
    def sum_bufs(wa, wb):
        return [
            vmem((2, nz, NX - 1, 16, wa), BF16),
            vmem((2, nz - 1, 16, wa), BF16),
            vmem((2, NX, nz - 1, 16, wb), BF16),
            vmem((2, NX - 1, 16, wb), BF16),
        ]

    results = pl.pallas_call(
        functools.partial(kernel, nz),
        out_shape=(
            jax.ShapeDtypeStruct((tok, share), BF16),
            jax.ShapeDtypeStruct((tok, share), F32),
            jax.ShapeDtypeStruct(w_in.shape, F32),
            jax.ShapeDtypeStruct(w_out.shape[::-1], F32),
        ),
        in_specs=[
            pl.BlockSpec(memory_space=pl.ANY),
        ]
        * 5,
        out_specs=[pl.BlockSpec(memory_space=pl.ANY)] * 4,
        scratch_shapes=[
            pltpu.SMEM(lengths.shape, lengths.dtype),
            vmem(w_in.shape, BF16),
            vmem(w_out.shape[::-1], BF16),
            vmem((tok, share), BF16),
            vmem((tok, share), F32),
            vmem(w_in.shape, F32),
            vmem(w_out.shape[::-1], F32),
            vmem((NY, tok, share), BF16),
            vmem((NY, tok, share), BF16),
            vmem((tok, width), BF16),
            vmem((NX, nz, 2, 16, tok), BF16),
            vmem((NX, nz, 2, 16, tok), BF16),
            vmem((NX, nz, 2, 16, COLS), BF16),
            vmem((tok, cols), F32),
            vmem((tok, cols), F32),
            vmem((tok, cols), BF16),
            vmem((tok, tok), F32),
            vmem((2, tok, tok), BF16),
            vmem((2, tok, tok), F32),
            vmem((tok, 2 * DH), F32),
            vmem((tok, 2 * DH), F32),
            vmem((tok, 2 * DH), BF16),
            vmem((tok, 2 * DH), BF16),
            vmem((tok, cols), BF16),
            vmem((2, tok, tok), BF16),
            vmem((NX, nz, 16, COLS), F32),
            vmem((NX, nz, 16, COLS), BF16),
            vmem((NX, nz, 16, COLS), BF16),
            vmem((NY, tok, share), F32),
            vmem((NY, tok, share), F32),
            vmem((2, tok, 128), F32),
            vmem((3, 8, tok), F32),
            vmem((3, NY, 8, tok), F32),
            vmem((6, half, share), BF16),
            vmem((6, half, share), BF16),
            vmem((6, half, share), BF16),
            vmem((6, half, share), BF16),
            sum_bufs(384, 128),
            sum_bufs(256, 128),
            sum_bufs(256, 128),
            pltpu.SemaphoreType.DMA((N_SEM,)),
            pltpu.SemaphoreType.DMA((N_SEM,)),
            pltpu.SemaphoreType.DMA((9,)),
        ],
        compiler_params=pltpu.CompilerParams(
            collective_id=0, has_side_effects=True, vmem_limit_bytes=60 * 1024 * 1024
        ),
    )(history, out_grad, lengths, w_in, w_out.T)
    anywhere = pl.BlockSpec(memory_space=pl.ANY)
    output, grad_input, grad_w_in, grad_w_out = pl.pallas_call(
        place_kernel,
        out_shape=[jax.ShapeDtypeStruct(r.shape, r.dtype) for r in results],
        in_specs=[anywhere] * 4,
        out_specs=[anywhere] * 4,
        scratch_shapes=[vmem(r.shape, r.dtype) for r in results] + [pltpu.SemaphoreType.DMA((8,))],
    )(*results)
    return output, grad_input, grad_w_in, grad_w_out.T


def solution(mesh):
    nz = mesh.shape["dp"] // (2 * NX)
    in_specs = (
        P("dp", "inner"),
        P("dp", "inner"),
        P("dp", None),
        P("dp", "inner"),
        P("inner", "dp"),
    )
    out_specs = (P("dp", "inner"), P("dp", "inner"), P("dp", "inner"), P("inner", "dp"))
    return jax.shard_map(
        functools.partial(shards, nz), mesh=mesh, in_specs=in_specs, out_specs=out_specs, check_vma=False
    )
```
